512 devices in a mesh: section: 8 (over x, core), dp: 32 (over y_hi, z), tensor: 2 (over y_lo).
Axes of the slice: x: 4, y: 8 (y_hi: 4, y_lo: 2; y = y_hi * 2 + y_lo), z: 8, core: 2. Of those that a mesh axis runs over, the one named last changes fastest.
Arguments:
- embeddings: bfloat16 [4096, 1024], P('dp'), may hold values from -6 to 6
- cotangent: bfloat16 [4096, 1024], P('dp'), may hold values from -6 to 6
- w_up: bfloat16 [8, 1024, 2048], P('section', 'dp', 'tensor'), may hold values from -0.1875 to 0.1875
- w_down: bfloat16 [8, 2048, 1024], P('section', 'tensor', 'dp'), may hold values from -0.125 to 0.125
- b_up: float32 [8, 2048], P('section', 'tensor'), may hold values from -3 to 3
- b_down: float32 [8, 1024], P('section'), may hold values from -3 to 3
- ln_gain: float32 [8, 1024], P('section'), may hold values from 0.5 to 1.5
- ln_bias: float32 [8, 1024], P('section'), may hold values from -2 to 2
- fwd_store: bfloat16 [8, 64, 128, 1024], P('section', 'dp'), may hold values from -6 to 6
- bwd_store: bfloat16 [8, 64, 128, 1024], P('section', 'dp'), may hold values from -6 to 6
- sample_ids: int32 [32], P('dp'), may hold values from 0 to 1
- fwd_scales: int32 [8, 4096, 8], P('section', 'dp'), may hold values from 1 to 8
- bwd_scales: int32 [8, 4096, 8], P('section', 'dp'), may hold values from 1 to 8
Outputs:
- layer_outs: bfloat16 [8, 4096, 1024], P('section', 'dp')
- input_grads: bfloat16 [8, 4096, 1024], P('section', 'dp')
- grad_up: float32 [8, 1024, 2048], P('section', 'dp', 'tensor')
- grad_down_t: float32 [8, 1024, 2048], P('section', 'dp', 'tensor')
The draws below stay inside these ranges and needn't reach their ends.
All inputs are finite; a program needn't handle non-finite values.
Results may differ from the reference program's by a relative error of at most 0.035.
Values may be sent and summed in bfloat16 or wider, within the bound.
A program may use at most 64 MiB of HBM per device.

```python
import jax
import jax.numpy as jnp
from jax import lax

D = 1024
FF = 2048
SEQ = 128
BLOCK = 128
MICRO = 1
STORE = 2
N_LAYERS = 8
TOK_DEV = 128
TOKENS = 4096
SAMPLES = 64
N_DP = 32


def touch_ends(values, stream_key, smallest, high):
    longest = values.shape.index(max(values.shape))
    spots = []
    for shift in (0, 1):
        where = [jax.random.randint(jax.random.fold_in(stream_key, axis), (), 0, length) for axis, length in enumerate(values.shape)]
        where[longest] = (where[longest] + shift) % values.shape[longest]
        spots.append(tuple(where))
    return values.at[spots[0]].set(smallest).at[spots[1]].set(high)


def block_scale(rng, dims, cuts, smallest, high):
    def one(dim, blocks):
        heights = jax.random.uniform(jax.random.fold_in(jax.random.fold_in(rng, 6), dim), (blocks,), jnp.float32, smallest / len(cuts), high / len(cuts))
        return jnp.repeat(jnp.exp(heights), dims[dim] // blocks).reshape((-1,) + (1,) * (len(dims) - dim - 1))

    gain = one(*cuts[0])
    for cut in cuts[1:]:
        gain = gain * one(*cut)
    return gain


def gaussian(rng, dims, scale, reach, pieces=(), held_as=jnp.bfloat16):
    gain = block_scale(rng, dims, pieces, -0.22, 0.18) if pieces else 1.0
    values = jax.random.normal(rng, dims, jnp.float32) * scale * gain
    return jnp.minimum(jnp.maximum(values, -reach), reach).astype(held_as)


def setup_inputs(seed: int = 0) -> dict:
    key_of = jax.random.split(jax.random.key(seed), 14)
    embeddings = gaussian(key_of[0], (TOKENS, D), 1.0, 6.0, ((0, 32),))
    cotangent = gaussian(key_of[1], (TOKENS, D), 1.0, 6.0, ((0, 32),))
    w_up = gaussian(key_of[2], (N_LAYERS, D, FF), D ** -0.5, 0.1875, ((0, 8), (1, 32), (2, 2)))
    w_down = gaussian(key_of[3], (N_LAYERS, FF, D), FF ** -0.5, 0.125, ((0, 8), (1, 2), (2, 32)))
    b_up = gaussian(key_of[4], (N_LAYERS, FF), 0.5, 3.0, ((0, 8), (1, 2)), jnp.float32)
    b_down = gaussian(key_of[5], (N_LAYERS, D), 0.5, 3.0, ((0, 8),), jnp.float32)
    ln_gain = jnp.clip(1.0 + 0.1 * jax.random.normal(key_of[6], (N_LAYERS, D), jnp.float32), 0.5, 1.5)
    ln_bias = gaussian(key_of[7], (N_LAYERS, D), 0.3, 2.0, ((0, 8),), jnp.float32)
    fwd_store = gaussian(key_of[8], (N_LAYERS, SAMPLES, SEQ, D), 1.0, 6.0, ((0, 8), (1, 32)))
    bwd_store = gaussian(key_of[9], (N_LAYERS, SAMPLES, SEQ, D), 1.0, 6.0, ((0, 8), (1, 32)))
    sample_ids = touch_ends(jax.random.randint(key_of[10], (N_DP * MICRO,), 0, STORE), jax.random.fold_in(key_of[10], 1), 0, STORE - 1).astype(jnp.int32)
    fwd_scales = touch_ends(jax.random.randint(key_of[11], (N_LAYERS, TOKENS, D // BLOCK), 1, 9), jax.random.fold_in(key_of[11], 1), 1, 8).astype(jnp.int32)
    bwd_scales = touch_ends(jax.random.randint(key_of[12], (N_LAYERS, TOKENS, D // BLOCK), 1, 9), jax.random.fold_in(key_of[12], 1), 1, 8).astype(jnp.int32)
    return {"embeddings": embeddings, "cotangent": cotangent, "w_up": w_up, "w_down": w_down, "b_up": b_up, "b_down": b_down, "ln_gain": ln_gain, "ln_bias": ln_bias, "fwd_store": fwd_store, "bwd_store": bwd_store, "sample_ids": sample_ids, "fwd_scales": fwd_scales, "bwd_scales": bwd_scales}


root_half = 0.7071067811865476
density = 0.3989422804014327
epsilon = 1e-05

def gelu_value(pre_gelu):
    return pre_gelu * 0.5 * (1.0 + lax.erf(pre_gelu * root_half))

def gelu_slope(pre_gelu):
    return 0.5 * (1.0 + lax.erf(pre_gelu * root_half)) + pre_gelu * jnp.exp(-0.5 * pre_gelu * pre_gelu) * density

def normalize(inputs):
    values = inputs.astype(jnp.float32)
    centered = values - lax.optimization_barrier(jnp.mean(values, axis=-1, keepdims=True))
    inverse = lax.rsqrt(lax.optimization_barrier(jnp.mean(centered * centered, axis=-1, keepdims=True)) + epsilon)
    return (centered * inverse, inverse)

def norm_backward(inputs, norm_gain, upstream):
    unit_values, inverse = normalize(inputs)
    scaled = upstream * norm_gain
    first_mean = lax.optimization_barrier(jnp.mean(scaled, axis=-1, keepdims=True))
    second_mean = lax.optimization_barrier(jnp.mean(scaled * unit_values, axis=-1, keepdims=True))
    return inverse * (scaled - first_mean - unit_values * second_mean)

def coded(values, stored_rows, scale_rows):
    block_count = scale_rows.shape[-1]
    bound_rows = 0.25 * jnp.repeat(scale_rows.astype(jnp.float32), values.shape[-1] // block_count, axis=-1)
    base_values = stored_rows.astype(jnp.float32)
    return (base_values + jnp.clip(values.astype(jnp.float32) - base_values, -bound_rows, bound_rows)).astype(jnp.bfloat16)

def inner(left, right):
    return lax.dot_general(left, right, (((0,), (0,)), ((), ())), preferred_element_type=jnp.float32)

def outer_t(left, right):
    return lax.dot_general(left, right, (((1,), (1,)), ((), ())), preferred_element_type=jnp.float32)

def rounded(values):
    narrow = lax.optimization_barrier(values.astype(jnp.bfloat16))
    return narrow.astype(jnp.float32)

def group_grads(normed, pre_grad, activated, upstream):

    def shaped(array):
        return array.reshape(N_DP, TOK_DEV, array.shape[-1])

    def add_group(totals, item):
        normed_rows, pre_rows, act_rows, up_rows = item
        up_term = rounded(inner(normed_rows, pre_rows))
        down_term = rounded(inner(up_rows, act_rows))
        return ((totals[0] + up_term, totals[1] + down_term), None)
    start_sums = (jnp.zeros((D, FF), jnp.float32), jnp.zeros((D, FF), jnp.float32))
    sums, _ = lax.scan(add_group, start_sums, (shaped(normed), shaped(pre_grad), shaped(activated), shaped(upstream)))
    return sums

def reference(embeddings, cotangent, w_up, w_down, b_up, b_down, ln_gain, ln_bias, fwd_store, bwd_store, sample_ids, fwd_scales, bwd_scales):
    group_ids = jnp.arange(N_DP * MICRO, dtype=jnp.int32) // MICRO
    store_rows = (group_ids * STORE + sample_ids).astype(jnp.int32)

    def stored(store):
        return jnp.take(store, store_rows, axis=0).reshape(TOKENS, D)

    def forward_parts(inputs, layer):
        unit_values, _ = normalize(inputs)
        normed = (unit_values * ln_gain[layer] + ln_bias[layer]).astype(jnp.bfloat16)
        pre_gelu = jnp.dot(normed, w_up[layer], preferred_element_type=jnp.float32) + b_up[layer]
        activated = gelu_value(pre_gelu).astype(jnp.bfloat16)
        return (normed, pre_gelu, activated)
    inputs = embeddings
    input_list = []
    output_list = []
    for layer in range(N_LAYERS):
        normed, pre_gelu, activated = forward_parts(inputs, layer)
        summed = jnp.dot(activated, w_down[layer], preferred_element_type=jnp.float32)
        output = (inputs.astype(jnp.float32) + summed + b_down[layer]).astype(jnp.bfloat16)
        input_list.append(inputs)
        output_list.append(output)
        inputs = coded(output, stored(fwd_store[layer]), fwd_scales[layer])
    upstream = cotangent
    grad_list = [None] * N_LAYERS
    up_list = [None] * N_LAYERS
    down_list = [None] * N_LAYERS
    for layer in reversed(range(N_LAYERS)):
        inputs = input_list[layer]
        normed, pre_gelu, activated = forward_parts(inputs, layer)
        act_grad = outer_t(upstream, w_down[layer])
        pre_grad = (act_grad * gelu_slope(pre_gelu)).astype(jnp.bfloat16)
        norm_grad = outer_t(pre_grad, w_up[layer])
        input_grad = (upstream.astype(jnp.float32) + norm_backward(inputs, ln_gain[layer], norm_grad)).astype(jnp.bfloat16)
        up_sum, down_sum = group_grads(normed, pre_grad, activated, upstream)
        grad_list[layer] = input_grad
        up_list[layer] = up_sum
        down_list[layer] = down_sum
        upstream = coded(input_grad, stored(bwd_store[layer]), bwd_scales[layer])
    return (jnp.stack(output_list), jnp.stack(grad_list), jnp.stack(up_list), jnp.stack(down_list))
```

```python
import functools

import jax
import jax.numpy as jnp
from jax import lax
from jax.experimental import pallas as pl
from jax.experimental.pallas import tpu as pltpu
from jax.sharding import PartitionSpec as P

MESH = pl.DeviceIdType.MESH
BF16 = jnp.bfloat16
F32 = jnp.float32
Y_LO = 2
Y_HI = 4

root_half = 0.7071067811865476
density = 0.3989422804014327
epsilon = 1e-05


class Place:
    def __init__(self, n_dp, y_hi=Y_HI):
        self.y_hi_n = y_hi
        self.z_n = n_dp // y_hi
        self.y_n = y_hi * Y_LO
        self.dp = lax.axis_index("dp")
        self.lo = lax.axis_index("tensor")
        self.hi = self.dp // self.z_n
        self.z = self.dp % self.z_n
        self.y = self.hi * Y_LO + self.lo

    def at_y(self, y):
        return {"dp": (y // Y_LO) * self.z_n + self.z, "tensor": y % Y_LO}

    def at_z(self, z):
        return {"dp": self.hi * self.z_n + z, "tensor": self.lo}

    def step_y(self, d):
        return (self.y + d + self.y_n) % self.y_n

    def step_z(self, d):
        return (self.z + d + self.z_n) % self.z_n


def signal(barrier, device_id):
    pl.semaphore_signal(barrier, inc=1, device_id=device_id, device_id_type=MESH)


def remote(src, dst, send_sem, recv_sem, device_id):
    return pltpu.make_async_remote_copy(
        src_ref=src, dst_ref=dst, send_sem=send_sem, recv_sem=recv_sem, device_id=device_id, device_id_type=MESH
    )


class Ring:
    def __init__(self, n, step, slot, device, send_sem, recv_sem):
        self.n, self.step, self.slot, self.device = n, step, slot, device
        self.send_sem, self.recv_sem = send_sem, recv_sem
        self.rounds = n // 2
        self.copies = {}

    def start(self, r):
        last = r == self.rounds - 1
        for way, sign in ((0, 1), (1, -1)):
            block = self.slot(self.step(-sign * r), way if last else None)
            copy = remote(
                block, block, self.send_sem.at[way, r], self.recv_sem.at[way, r], self.device(self.step(sign))
            )
            copy.start()
            self.copies[way, r] = copy

    def wait_recv(self, r):
        last = r == self.rounds - 1
        for way, sign in ((0, 1), (1, -1)):
            block = self.slot(self.step(-sign * (r + 1)), way if last else None)
            remote(
                block, block, self.send_sem.at[way, r], self.recv_sem.at[way, r], self.device(self.step(sign))
            ).wait_recv()

    def wait_send(self):
        for copy in self.copies.values():
            copy.wait_send()


def run_rings(rings):
    for r in range(max(ring.rounds for ring in rings)):
        live = [ring for ring in rings if r < ring.rounds]
        for ring in live:
            ring.start(r)
        for ring in live:
            ring.wait_recv(r)


def half_of(ref, part, size):
    return ref if part is None else ref.at[pl.ds(part * (size // 2), size // 2)]


def gather_kernel(
    n_dp, y_hi, up_ref, down_ref, bias_ref, up_all, down_all, bias_all, send_sem, recv_sem, bias_sem
):
    at = Place(n_dp, y_hi)
    rows = up_ref.shape[0]
    peer = {"tensor": 1 - at.lo}
    barrier = pltpu.get_barrier_semaphore()
    for d in (1, -1):
        signal(barrier, at.at_y(at.step_y(d)))
        signal(barrier, at.at_z(at.step_z(d)))
    up_all[at.lo, at.hi, at.z] = up_ref[...]
    down_all[at.lo, at.hi, at.z] = down_ref[...]
    bias_all[at.lo] = bias_ref[...]
    pl.semaphore_wait(barrier, 4)

    bias_copy = remote(bias_all.at[at.lo], bias_all.at[at.lo], bias_sem.at[0], bias_sem.at[1], peer)
    bias_copy.start()

    def up_block(y, part):
        return half_of(up_all.at[y % Y_LO, y // Y_LO, at.z], part, rows)

    def down_block(z, part):
        return half_of(down_all.at[at.lo, at.hi, z], part, rows)

    def up_column(z, part):
        if part is None:
            return up_all.at[:, :, z]
        return up_all.at[part, :, z]

    def down_row(y, part):
        return half_of(down_all.at[y % Y_LO, y // Y_LO], part, at.z_n)

    first = [
        Ring(at.y_n, at.step_y, up_block, at.at_y, send_sem.at[0], recv_sem.at[0]),
        Ring(at.z_n, at.step_z, down_block, at.at_z, send_sem.at[1], recv_sem.at[1]),
    ]
    run_rings(first)
    second = [
        Ring(at.z_n, at.step_z, up_column, at.at_z, send_sem.at[2], recv_sem.at[2]),
        Ring(at.y_n, at.step_y, down_row, at.at_y, send_sem.at[3], recv_sem.at[3]),
    ]
    run_rings(second)
    for ring in first + second:
        ring.wait_send()
    remote(
        bias_all.at[1 - at.lo], bias_all.at[1 - at.lo], bias_sem.at[0], bias_sem.at[1], peer
    ).wait_recv()
    bias_copy.wait_send()


def gelu_value(pre_gelu):
    return pre_gelu * 0.5 * (1.0 + lax.erf(pre_gelu * root_half))


def gelu_slope(pre_gelu):
    return (
        0.5 * (1.0 + lax.erf(pre_gelu * root_half))
        + pre_gelu * jnp.exp(-0.5 * pre_gelu * pre_gelu) * density
    )


def outer_t(left, right):
    return lax.dot_general(left, right, (((1,), (1,)), ((), ())), preferred_element_type=F32)


def inner(left, right):
    return lax.dot_general(left, right, (((0,), (0,)), ((), ())), preferred_element_type=F32)


def coded(values, base, bound):
    base = base.astype(F32)
    return (base + jnp.clip(values.astype(F32) - base, -bound, bound)).astype(BF16)


def chain_kernel(
    n_sections,
    tile,
    sid_ref,
    emb_ref,
    cot_ref,
    fst_ref,
    bst_ref,
    fsc_ref,
    bsc_ref,
    gain_ref,
    bias_ref,
    bdown_ref,
    bup_ref,
    wu_ref,
    wd_ref,
    out_ref,
    ig_ref,
    normed_ref,
    act_ref,
    pg_ref,
    g_ref,
    x_in,
    code_f,
    code_b,
    bound_f,
    bound_b,
    slope,
    unit,
    inv,
    scaled,
    fwd_send,
    fwd_recv,
    bwd_send,
    bwd_recv,
    peer_send,
    peer_recv,
):
    section = lax.axis_index("section")
    lo = lax.axis_index("tensor")
    rows, width = x_in.shape
    half = wu_ref.shape[2]
    tiles = half // tile
    wide = min(width, 256)
    d_tiles = width // wide
    mine = pl.ds(pl.multiple_of(lo * rows, rows), rows)
    not_first = section > 0
    not_last = section < n_sections - 1
    after = {"section": jnp.minimum(section + 1, n_sections - 1)}
    before = {"section": jnp.maximum(section - 1, 0)}
    peer = {"tensor": 1 - lo}

    barrier = pltpu.get_barrier_semaphore()
    signal(barrier, peer)

    @pl.when(not_first)
    def _():
        signal(barrier, before)

    @pl.when(not_last)
    def _():
        signal(barrier, after)

    sid = sid_ref[0]
    block = width // fsc_ref.shape[1]
    for b in range(fsc_ref.shape[1]):
        cols = pl.ds(b * block, block)
        bound_f[:, cols] = jnp.broadcast_to(0.25 * fsc_ref[mine, b : b + 1].astype(F32), (rows, block))
        bound_b[:, cols] = jnp.broadcast_to(0.25 * bsc_ref[mine, b : b + 1].astype(F32), (rows, block))

    @pl.when(section == 0)
    def _():
        x_in[...] = emb_ref[mine, :]

    @pl.when(jnp.logical_not(not_last))
    def _():
        g_ref[...] = cot_ref[mine, :]

    pl.semaphore_wait(barrier, 1 + not_first.astype(jnp.int32) + not_last.astype(jnp.int32))

    def columns(j):
        return pl.ds(pl.multiple_of(j * wide, wide), wide)

    def fwd_copy(j):
        return remote(code_f.at[:, columns(j)], x_in.at[:, columns(j)], fwd_send.at[j], fwd_recv.at[j], after)

    def bwd_copy(j):
        return remote(code_b.at[:, columns(j)], g_ref.at[:, columns(j)], bwd_send.at[j], bwd_recv.at[j], before)

    @pl.when(not_first)
    def _():
        for j in range(d_tiles):
            fwd_copy(j).wait_recv()

    values = x_in[...].astype(F32)
    centered = values - jnp.mean(values, axis=-1, keepdims=True)
    inverse = lax.rsqrt(jnp.mean(centered * centered, axis=-1, keepdims=True) + epsilon)
    unit_values = centered * inverse
    normed_ref[...] = (unit_values * gain_ref[...] + bias_ref[...]).astype(BF16)
    unit[...] = unit_values
    inv[...] = jnp.broadcast_to(inverse, inv.shape)

    def up_tile(j, _):
        h, c = j // tiles, j % tiles
        cols = pl.ds(pl.multiple_of(c * tile, tile), tile)
        spot = pl.ds(pl.multiple_of(j * tile, tile), tile)
        pre = jnp.dot(normed_ref[...], wu_ref[h, :, cols], preferred_element_type=F32) + bup_ref[h, 0:1, cols]
        slope[:, spot] = pre
        act_ref[:, spot] = gelu_value(pre).astype(BF16)
        return 0

    lax.fori_loop(0, 2 * tiles, up_tile, 0)

    def down_tile(j, _):
        cols = columns(j)
        total = outer_t(act_ref[:, :half], wd_ref[0, cols, :]) + outer_t(act_ref[:, half:], wd_ref[1, cols, :])
        output = (x_in[:, cols].astype(F32) + total + bdown_ref[:, cols]).astype(BF16)
        out_ref[mine, cols] = output
        code_f[:, cols] = coded(output, fst_ref[sid, mine, cols], bound_f[:, cols])

        @pl.when(not_last)
        def _():
            fwd_copy(j).start()

        return 0

    lax.fori_loop(0, d_tiles, down_tile, 0)
    out_copy = remote(out_ref.at[mine], out_ref.at[mine], peer_send.at[0], peer_recv.at[0], peer)
    out_copy.start()

    def slope_tile(j, _):
        spot = pl.ds(pl.multiple_of(j * tile, tile), tile)
        slope[:, spot] = gelu_slope(slope[:, spot])
        return 0

    lax.fori_loop(0, 2 * tiles, slope_tile, 0)

    @pl.when(not_last)
    def _():
        for j in range(d_tiles):
            fwd_copy(j).wait_send()
        for j in range(d_tiles):
            bwd_copy(j).wait_recv()

    def up_grad_tile(j, _):
        h, c = j // tiles, j % tiles
        cols = pl.ds(pl.multiple_of(c * tile, tile), tile)
        spot = pl.ds(pl.multiple_of(j * tile, tile), tile)
        act_grad = jnp.dot(g_ref[...], wd_ref[h, :, cols], preferred_element_type=F32)
        pg_ref[:, spot] = (act_grad * slope[:, spot]).astype(BF16)
        return 0

    lax.fori_loop(0, 2 * tiles, up_grad_tile, 0)

    def norm_grad_tile(j, _):
        cols = columns(j)
        total = outer_t(pg_ref[:, :half], wu_ref[0, cols, :]) + outer_t(pg_ref[:, half:], wu_ref[1, cols, :])
        scaled[:, cols] = total * gain_ref[:, cols]
        return 0

    lax.fori_loop(0, d_tiles, norm_grad_tile, 0)
    scaled_values = scaled[...]
    unit_values = unit[...]
    first_mean = jnp.mean(scaled_values, axis=-1, keepdims=True)
    second_mean = jnp.mean(scaled_values * unit_values, axis=-1, keepdims=True)

    for j in range(d_tiles):
        cols = columns(j)
        inner_part = scaled[:, cols] - first_mean - unit[:, cols] * second_mean
        input_grad = (g_ref[:, cols].astype(F32) + inv[:, 0:1] * inner_part).astype(BF16)
        ig_ref[mine, cols] = input_grad
        code_b[:, cols] = coded(input_grad, bst_ref[sid, mine, cols], bound_b[:, cols])

        @pl.when(not_first)
        def _():
            bwd_copy(j).start()

    ig_copy = remote(ig_ref.at[mine], ig_ref.at[mine], peer_send.at[1], peer_recv.at[1], peer)
    ig_copy.start()

    @pl.when(not_first)
    def _():
        for j in range(d_tiles):
            bwd_copy(j).wait_send()

    other = pl.ds(pl.multiple_of((1 - lo) * rows, rows), rows)
    remote(out_ref.at[other], out_ref.at[other], peer_send.at[0], peer_recv.at[0], peer).wait_recv()
    remote(ig_ref.at[other], ig_ref.at[other], peer_send.at[1], peer_recv.at[1], peer).wait_recv()
    out_copy.wait_send()
    ig_copy.wait_send()


def grads_kernel(
    n_dp,
    y_hi,
    normed_ref,
    act_ref,
    pg_ref,
    g_ref,
    up_out,
    down_out,
    normed_all,
    act_all,
    pg_all,
    g_all,
    up_block,
    down_block,
    ex_send,
    ex_recv,
    ring_send,
    ring_recv,
    out_send,
    out_recv,
):
    at = Place(n_dp, y_hi)
    rows = normed_ref.shape[0]
    features = normed_all.shape[3]
    hidden = act_all.shape[3]
    out_rows = up_out.shape[0]
    owner_z = at.dp // at.y_hi_n

    barrier = pltpu.get_barrier_semaphore()
    for d in range(1, at.y_n):
        signal(barrier, at.at_y(at.step_y(d)))
    for d in range(1, at.z_n):
        signal(barrier, at.at_z(at.step_z(d)))
    for i in range(at.y_hi_n):
        source = i * at.z_n + owner_z
        target = at.z * at.y_hi_n + i

        @pl.when(source != at.dp)
        def _():
            signal(barrier, {"dp": source})

    sends_self = jnp.int32(0)
    for i in range(at.y_hi_n):
        sends_self = sends_self + (at.z * at.y_hi_n + i == at.dp).astype(jnp.int32)
    pl.semaphore_wait(barrier, at.y_n + at.z_n - 2 + at.y_hi_n - sends_self)

    def feature_cols(z):
        return pl.ds(pl.multiple_of(z * features, features), features)

    def hidden_cols(y):
        spot = (y % Y_LO) * at.y_hi_n + y // Y_LO
        return pl.ds(pl.multiple_of(spot * hidden, hidden), hidden)

    def z_copy(k, src, dst, d):
        target = at.step_z(d)
        return remote(
            src.at[:, feature_cols(target)], dst.at[at.y, at.z], ex_send.at[k, d], ex_recv.at[k, d], at.at_z(target)
        )

    def y_copy(k, src, dst, d):
        target = at.step_y(d)
        return remote(
            src.at[:, hidden_cols(target)], dst.at[at.y, at.z], ex_send.at[k, d], ex_recv.at[k, d], at.at_y(target)
        )

    z_parts = ((0, normed_ref, normed_all), (1, g_ref, g_all))
    y_parts = ((2, act_ref, act_all), (3, pg_ref, pg_all))
    for d in range(1, at.y_n):
        for k, src, dst in y_parts:
            y_copy(k, src, dst, d).start()
    for d in range(1, at.z_n):
        for k, src, dst in z_parts:
            z_copy(k, src, dst, d).start()
    for k, src, dst in z_parts:
        dst[at.y, at.z] = src[:, feature_cols(at.z)]
    for k, src, dst in y_parts:
        dst[at.y, at.z] = src[:, hidden_cols(at.y)]
    for d in range(1, at.y_n):
        for k, src, dst in y_parts:
            spot = dst.at[at.step_y(-d), at.z]
            remote(spot, spot, ex_send.at[k, d], ex_recv.at[k, d], at.at_y(at.step_y(d))).wait_recv()
    for d in range(1, at.z_n):
        for k, src, dst in z_parts:
            spot = dst.at[at.y, at.step_z(-d)]
            remote(spot, spot, ex_send.at[k, d], ex_recv.at[k, d], at.at_z(at.step_z(d))).wait_recv()

    def row_slot(ref):
        return lambda y, part: half_of(ref.at[y], part, at.z_n)

    def column_slot(ref):
        half = at.y_n // 2

        def slot(z, part):
            if part is None:
                return ref.at[:, z]
            return ref.at[pl.ds(part * half, half), z]

        return slot

    rings = [
        Ring(at.z_n, at.step_z, column_slot(pg_all), at.at_z, ring_send.at[3], ring_recv.at[3]),
        Ring(at.z_n, at.step_z, column_slot(act_all), at.at_z, ring_send.at[2], ring_recv.at[2]),
        Ring(at.y_n, at.step_y, row_slot(normed_all), at.at_y, ring_send.at[0], ring_recv.at[0]),
        Ring(at.y_n, at.step_y, row_slot(g_all), at.at_y, ring_send.at[1], ring_recv.at[1]),
    ]
    run_rings(rings)

    tokens = at.z_n * rows

    def accumulate(block, left, right):
        block[...] = jnp.zeros_like(block)

        def body(y, _):
            block[...] += inner(left[y].reshape(tokens, features), right[y].reshape(tokens, hidden))
            return 0

        lax.fori_loop(0, at.y_n, body, 0)

    accumulate(up_block, normed_all, pg_all)
    accumulate(down_block, g_all, act_all)

    out_cols = pl.ds(pl.multiple_of(at.hi * hidden, hidden), hidden)

    def out_copy(k, block, out, i):
        return remote(
            block.at[pl.ds(i * out_rows, out_rows)],
            out.at[:, out_cols],
            out_send.at[k, i],
            out_recv.at[k, at.hi],
            {"dp": at.z * at.y_hi_n + i},
        )

    outs = ((0, up_block, up_out), (1, down_block, down_out))
    for i in range(at.y_hi_n):
        own = at.z * at.y_hi_n + i == at.dp

        @pl.when(jnp.logical_not(own))
        def _():
            for k, block, out in outs:
                out_copy(k, block, out, i).start()

        @pl.when(own)
        def _():
            for k, block, out in outs:
                out[:, out_cols] = block[pl.ds(i * out_rows, out_rows), :]

    for i in range(at.y_hi_n):

        @pl.when(i * at.z_n + owner_z != at.dp)
        def _():
            for k, block, out in outs:
                spot = out.at[:, pl.ds(i * hidden, hidden)]
                remote(spot, spot, out_send.at[k, 0], out_recv.at[k, i], {"dp": at.z * at.y_hi_n + i}).wait_recv()

    for i in range(at.y_hi_n):

        @pl.when(at.z * at.y_hi_n + i != at.dp)
        def _():
            for k, block, out in outs:
                out_copy(k, block, out, i).wait_send()

    for d in range(1, at.y_n):
        for k, src, dst in y_parts:
            y_copy(k, src, dst, d).wait_send()
    for d in range(1, at.z_n):
        for k, src, dst in z_parts:
            z_copy(k, src, dst, d).wait_send()
    for ring in rings:
        ring.wait_send()


def vmem(count):
    return [pl.BlockSpec(memory_space=pltpu.VMEM)] * count


def params(collective_id, limit=56):
    return pltpu.CompilerParams(
        collective_id=collective_id, has_side_effects=True, vmem_limit_bytes=limit * 1024 * 1024
    )


def per_device(
    n_sections,
    n_dp,
    y_hi,
    embeddings,
    cotangent,
    w_up,
    w_down,
    b_up,
    b_down,
    ln_gain,
    ln_bias,
    fwd_store,
    bwd_store,
    sample_ids,
    fwd_scales,
    bwd_scales,
):
    z_n = n_dp // y_hi
    y_n = y_hi * Y_LO
    shard, half = w_up.shape[1:]
    width = embeddings.shape[1]
    rows = embeddings.shape[0] // Y_LO
    dma = pltpu.SemaphoreType.DMA
    rounds = max(y_n, z_n) // 2
    whole = jax.ShapeDtypeStruct((Y_LO, y_hi, z_n, shard, half), BF16)
    up_all, down_all, bias_all = pl.pallas_call(
        functools.partial(gather_kernel, n_dp, y_hi),
        out_shape=(whole, whole, jax.ShapeDtypeStruct((Y_LO, 8, half), F32)),
        in_specs=vmem(3),
        out_specs=tuple(vmem(3)),
        scratch_shapes=[dma((4, 2, rounds)), dma((4, 2, rounds)), dma((2,))],
        compiler_params=params(0),
    )(w_up[0], w_down[0].T, jnp.broadcast_to(b_up, (8, half)))
    up_all = up_all.reshape(Y_LO, width, half)
    down_all = down_all.reshape(Y_LO, width, half)

    d_tiles = width // min(width, 256)
    hidden_all = Y_LO * half
    out, ig, normed, act, pre_grad, upstream = pl.pallas_call(
        functools.partial(chain_kernel, n_sections, min(half, 512)),
        out_shape=(
            jax.ShapeDtypeStruct(embeddings.shape, BF16),
            jax.ShapeDtypeStruct(embeddings.shape, BF16),
            jax.ShapeDtypeStruct((rows, width), BF16),
            jax.ShapeDtypeStruct((rows, hidden_all), BF16),
            jax.ShapeDtypeStruct((rows, hidden_all), BF16),
            jax.ShapeDtypeStruct((rows, width), BF16),
        ),
        in_specs=[pl.BlockSpec(memory_space=pltpu.SMEM)] + vmem(12),
        out_specs=tuple(vmem(6)),
        scratch_shapes=[
            pltpu.VMEM((rows, width), BF16),
            pltpu.VMEM((rows, width), BF16),
            pltpu.VMEM((rows, width), BF16),
            pltpu.VMEM((rows, width), F32),
            pltpu.VMEM((rows, width), F32),
            pltpu.VMEM((rows, hidden_all), F32),
            pltpu.VMEM((rows, width), F32),
            pltpu.VMEM((rows, 128), F32),
            pltpu.VMEM((rows, width), F32),
            dma((d_tiles,)),
            dma((d_tiles,)),
            dma((d_tiles,)),
            dma((d_tiles,)),
            dma((2,)),
            dma((2,)),
        ],
        compiler_params=params(1),
    )(
        sample_ids,
        embeddings,
        cotangent,
        fwd_store[0],
        bwd_store[0],
        fwd_scales[0],
        bwd_scales[0],
        ln_gain,
        ln_bias,
        b_down,
        bias_all,
        up_all,
        down_all,
    )

    features = width // z_n
    hidden = hidden_all // y_n
    peers = max(y_n, z_n)
    grad_up, grad_down = pl.pallas_call(
        functools.partial(grads_kernel, n_dp, y_hi),
        out_shape=(jax.ShapeDtypeStruct((shard, half), F32), jax.ShapeDtypeStruct((shard, half), F32)),
        in_specs=vmem(4),
        out_specs=tuple(vmem(2)),
        scratch_shapes=[
            pltpu.VMEM((y_n, z_n, rows, features), BF16),
            pltpu.VMEM((y_n, z_n, rows, hidden), BF16),
            pltpu.VMEM((y_n, z_n, rows, hidden), BF16),
            pltpu.VMEM((y_n, z_n, rows, features), BF16),
            pltpu.VMEM((features, hidden), F32),
            pltpu.VMEM((features, hidden), F32),
            dma((4, peers)),
            dma((4, peers)),
            dma((4, 2, rounds)),
            dma((4, 2, rounds)),
            dma((2, y_hi)),
            dma((2, y_hi)),
        ],
        compiler_params=params(2),
    )(normed, act, pre_grad, upstream)
    return (out[None], ig[None], grad_up[None], grad_down[None])


def solution(mesh, y_hi=Y_HI):
    return jax.shard_map(
        functools.partial(per_device, mesh.shape["section"], mesh.shape["dp"], y_hi),
        mesh=mesh,
        in_specs=(
            P("dp", None),
            P("dp", None),
            P("section", "dp", "tensor"),
            P("section", "tensor", "dp"),
            P("section", "tensor"),
            P("section", None),
            P("section", None),
            P("section", None),
            P("section", "dp", None, None),
            P("section", "dp", None, None),
            P("dp"),
            P("section", "dp", None),
            P("section", "dp", None),
        ),
        out_specs=(
            P("section", "dp", None),
            P("section", "dp", None),
            P("section", "dp", "tensor"),
            P("section", "dp", "tensor"),
        ),
        check_vma=False,
    )
```

```python
import functools

import jax
import jax.numpy as jnp
from jax import lax
from jax.experimental import pallas as pl
from jax.experimental.pallas import tpu as pltpu
from jax.sharding import PartitionSpec as P

MESH = pl.DeviceIdType.MESH
BF16 = jnp.bfloat16
F32 = jnp.float32
Y_LO = 2
Y_HI = 4

root_half = 0.7071067811865476
density = 0.3989422804014327
epsilon = 1e-05


class Place:
    def __init__(self, n_dp, y_hi=Y_HI):
        self.y_hi_n = y_hi
        self.z_n = n_dp // y_hi
        self.y_n = y_hi * Y_LO
        self.dp = lax.axis_index("dp")
        self.lo = lax.axis_index("tensor")
        self.hi = self.dp // self.z_n
        self.z = self.dp % self.z_n
        self.y = self.hi * Y_LO + self.lo

    def at_y(self, y):
        return {"dp": (y // Y_LO) * self.z_n + self.z, "tensor": y % Y_LO}

    def at_z(self, z):
        return {"dp": self.hi * self.z_n + z, "tensor": self.lo}

    def step_y(self, d):
        return (self.y + d + self.y_n) % self.y_n

    def step_z(self, d):
        return (self.z + d + self.z_n) % self.z_n


def signal(barrier, device_id):
    pl.semaphore_signal(barrier, inc=1, device_id=device_id, device_id_type=MESH)


def remote(src, dst, send_sem, recv_sem, device_id):
    return pltpu.make_async_remote_copy(
        src_ref=src, dst_ref=dst, send_sem=send_sem, recv_sem=recv_sem, device_id=device_id, device_id_type=MESH
    )


class Ring:
    def __init__(self, n, step, slot, device, sems, index, last_way):
        self.step, self.slot, self.device = step, slot, device
        self.send_sem, self.recv_sem, self.index = sems[0], sems[1], index
        self.rounds = n // 2
        self.last_way = last_way

    def ways(self, r):
        return (self.last_way,) if r == self.rounds - 1 else (0, 1)

    def copy(self, way, r, received=False):
        sign = 1 - 2 * way
        block = self.slot(self.step(-sign * (r + 1 if received else r)))
        spot = (self.index, way, r)
        return remote(block, block, self.send_sem.at[spot], self.recv_sem.at[spot], self.device(self.step(sign)))

    def start(self, r):
        for way in self.ways(r):
            self.copy(way, r).start()

    def wait_recv(self, r):
        for way in self.ways(r):
            self.copy(way, r, True).wait_recv()

    def wait_send(self):
        for r in range(self.rounds):
            for way in self.ways(r):
                self.copy(way, r).wait_send()


def run_rings(rings, done=None):
    rounds = max(ring.rounds for ring in rings)
    for ring in rings:
        ring.start(0)
    for r in range(rounds):
        for ring in rings:
            if r < ring.rounds:
                ring.wait_recv(r)
                if r + 1 < ring.rounds:
                    ring.start(r + 1)
        if done is not None:
            done(r)


def run_gathers(pairs, lag=1.0):
    free, events, order = {}, [], []

    def push(ready, axis, ring, way, r, pair):
        begin = max(ready, free.get((axis, way), 0.0))
        free[axis, way] = begin + 1.0
        events.append((begin + 1.0 + lag, len(order) + len(events), ring, way, r, pair))
        return lambda: ring.copy(way, r).start()

    def begin_chunk(ready, pair, d):
        axis, ring = pair[2], pair[3][d]
        return [push(ready, axis, ring, way, 0, pair) for way in ring.ways(0)]

    starts = []
    for pair in pairs:
        starts += [push(0.0, pair[0], pair[1], way, 0, pair) for way in pair[1].ways(0)]
    for pair in pairs:
        starts += begin_chunk(0.0, pair, 0)
    for start in starts:
        start()
    while events:
        event = min(events, key=lambda e: e[:2])
        events.remove(event)
        order.append(event)
        now, _, ring, way, r, pair = event
        ring.copy(way, r, True).wait_recv()
        starts = []
        first = ring is pair[1]
        if r + 1 < ring.rounds and way in ring.ways(r + 1):
            starts.append(push(now, pair[0] if first else pair[2], ring, way, r + 1, pair))
        if first:
            starts += begin_chunk(now, pair, -(r + 1) if way == 0 else r + 1)
        for start in starts:
            start()


def gelu_value(pre_gelu):
    return pre_gelu * 0.5 * (1.0 + lax.erf(pre_gelu * root_half))


def gelu_slope(pre_gelu):
    return (
        0.5 * (1.0 + lax.erf(pre_gelu * root_half))
        + pre_gelu * jnp.exp(-0.5 * pre_gelu * pre_gelu) * density
    )


def outer_t(left, right):
    return lax.dot_general(left, right, (((1,), (1,)), ((), ())), preferred_element_type=F32)


def inner(left, right):
    return lax.dot_general(left, right, (((0,), (0,)), ((), ())), preferred_element_type=F32)


def coded(values, base, bound):
    base = base.astype(F32)
    return (base + jnp.clip(values.astype(F32) - base, -bound, bound)).astype(BF16)


def layer_kernel(
    n_sections,
    n_dp,
    y_hi,
    sid_ref,
    emb_ref,
    cot_ref,
    up_ref,
    down_ref,
    bup_ref,
    bdown_ref,
    gain_ref,
    bias_ref,
    fst_ref,
    bst_ref,
    fsc_ref,
    bsc_ref,
    out_ref,
    ig_ref,
    up_out,
    down_out,
    up_all,
    down_all,
    bias_all,
    x_in,
    g_in,
    fst,
    bst,
    normed,
    act,
    pre_grad,
    out_rows,
    ig_rows,
    code_f,
    code_b,
    bound_f,
    bound_b,
    slope,
    unit,
    inv,
    scaled,
    normed_all,
    act_all,
    pg_all,
    g_all,
    up_block,
    down_block,
    load_sem,
    bias_sem,
    hop_send,
    hop_recv,
    peer_send,
    peer_recv,
    ring_send,
    ring_recv,
    ex_send,
    ex_recv,
    out_send,
    out_recv,
):
    at = Place(n_dp, y_hi)
    section = lax.axis_index("section")
    rows, width = x_in.shape
    half = up_all.shape[4]
    features = normed_all.shape[3]
    hidden = act_all.shape[3]
    shard = up_ref.shape[0]
    wide = width // 2
    sems = (ring_send, ring_recv)
    mine = pl.ds(pl.multiple_of(at.lo * rows, rows), rows)
    other = pl.ds(pl.multiple_of((1 - at.lo) * rows, rows), rows)
    not_first = section > 0
    not_last = section < n_sections - 1
    early_first = section < n_sections // 2
    after = {"section": jnp.minimum(section + 1, n_sections - 1)}
    before = {"section": jnp.maximum(section - 1, 0)}
    peer = {"tensor": 1 - at.lo}
    owner_z = at.dp // at.y_hi_n

    barrier = pltpu.get_barrier_semaphore()
    for d in range(1, at.y_n):
        signal(barrier, at.at_y(at.step_y(d)))
    for d in range(1, at.z_n):
        signal(barrier, at.at_z(at.step_z(d)))
    for i in range(at.y_hi_n):
        source = i * at.z_n + owner_z

        @pl.when(source != at.dp)
        def _():
            signal(barrier, {"dp": source})

    @pl.when(not_first)
    def _():
        signal(barrier, before)

    @pl.when(not_last)
    def _():
        signal(barrier, after)

    own_up = pltpu.make_async_copy(up_ref, up_all.at[at.lo, at.hi, at.z], load_sem.at[0])
    own_down = pltpu.make_async_copy(down_ref, down_all.at[at.lo, at.hi, at.z], load_sem.at[1])
    load_fst = pltpu.make_async_copy(fst_ref.at[:, mine], fst, load_sem.at[2])
    load_bst = pltpu.make_async_copy(bst_ref.at[:, mine], bst, load_sem.at[3])
    load_emb = pltpu.make_async_copy(emb_ref.at[mine], x_in, load_sem.at[4])
    load_cot = pltpu.make_async_copy(cot_ref.at[mine], g_in, load_sem.at[5])
    own_up.start()
    own_down.start()
    load_fst.start()
    load_bst.start()

    @pl.when(section == 0)
    def _():
        load_emb.start()

    @pl.when(jnp.logical_not(not_last))
    def _():
        load_cot.start()

    bias_all[at.lo] = jnp.broadcast_to(bup_ref[...], bias_all.shape[1:])
    sends_self = jnp.int32(0)
    for i in range(at.y_hi_n):
        sends_self = sends_self + (at.z * at.y_hi_n + i == at.dp).astype(jnp.int32)
    sections_near = not_first.astype(jnp.int32) + not_last.astype(jnp.int32)
    own_up.wait()
    own_down.wait()
    pl.semaphore_wait(barrier, at.y_n + at.z_n - 2 + at.y_hi_n - sends_self + sections_near)

    bias_copy = remote(bias_all.at[at.lo], bias_all.at[at.lo], bias_sem.at[0], bias_sem.at[1], peer)
    bias_copy.start()

    def up_slot(y, z):
        return up_all.at[y % Y_LO, y // Y_LO, z]

    def down_slot(y, z):
        return down_all.at[y % Y_LO, y // Y_LO, z]

    def fixed(slot, axis, step, d):
        there = step(d)
        return (lambda z: slot(there, z)) if axis == "y" else (lambda y: slot(y, there))

    y_ring = (at.y_n, at.step_y)
    z_ring = (at.z_n, at.step_z)
    up_first = Ring(*y_ring, fixed(up_slot, "z", at.step_z, 0), at.at_y, sems, 0, 0)
    down_first = Ring(*z_ring, fixed(down_slot, "y", at.step_y, 0), at.at_z, sems, 1, 1)
    up_then, down_then = {}, {}
    index = 2
    for d in range(-(at.y_n // 2), at.y_n // 2):
        up_then[d] = Ring(*z_ring, fixed(up_slot, "y", at.step_y, d), at.at_z, sems, index, index % 2)
        index += 1
    for d in range(-(at.z_n // 2), at.z_n // 2):
        down_then[d] = Ring(*y_ring, fixed(down_slot, "z", at.step_z, d), at.at_y, sems, index, index % 2)
        index += 1
    if down_first.last_way == 1:
        down_then[at.z_n // 2] = down_then.pop(-(at.z_n // 2))
    weight_rings = [up_first, down_first, *up_then.values(), *down_then.values()]
    run_gathers((("y", up_first, "z", up_then), ("z", down_first, "y", down_then)))

    scale_f = jnp.transpose(fsc_ref[...].astype(F32))
    scale_b = jnp.transpose(bsc_ref[...].astype(F32))
    low = at.lo == 0
    scale_f = 0.25 * jnp.where(low, scale_f[:rows], scale_f[rows:])
    scale_b = 0.25 * jnp.where(low, scale_b[:rows], scale_b[rows:])
    for b in range(fsc_ref.shape[0]):
        block = width // fsc_ref.shape[0]
        cols = pl.ds(b * block, block)
        bound_f[:, cols] = jnp.broadcast_to(scale_f[:, b : b + 1], (rows, block))
        bound_b[:, cols] = jnp.broadcast_to(scale_b[:, b : b + 1], (rows, block))
    remote(bias_all.at[1 - at.lo], bias_all.at[1 - at.lo], bias_sem.at[0], bias_sem.at[1], peer).wait_recv()
    bias_copy.wait_send()
    load_fst.wait()
    load_bst.wait()
    sid = sid_ref[0]

    def columns(j):
        return pl.ds(pl.multiple_of(j * wide, wide), wide)

    def up_weights(h):
        return up_all[h].reshape(width, half)

    def down_weights(h):
        return down_all[h].reshape(width, half)

    def quarter(ref, h, j):
        count = y_hi // 2
        return ref[h, pl.ds(j * count, count)].reshape(wide, half)

    def fwd_copy(j):
        return remote(code_f.at[:, columns(j)], x_in.at[:, columns(j)], hop_send.at[0, j], hop_recv.at[0, j], after)

    def bwd_copy(j):
        return remote(code_b.at[:, columns(j)], g_in.at[:, columns(j)], hop_send.at[1, j], hop_recv.at[1, j], before)

    def hidden_half(h):
        return pl.ds(pl.multiple_of(h * half, half), half)

    def feature_cols(z):
        return pl.ds(pl.multiple_of(z * features, features), features)

    def hidden_cols(y):
        spot = (y % Y_LO) * at.y_hi_n + y // Y_LO
        return pl.ds(pl.multiple_of(spot * hidden, hidden), hidden)

    def z_copy(k, src, dst, d):
        target = at.step_z(d)
        return remote(
            src.at[:, feature_cols(target)], dst.at[at.y, at.z], ex_send.at[k, d], ex_recv.at[k, d], at.at_z(target)
        )

    def y_copy(k, src, dst, d):
        target = at.step_y(d)
        return remote(
            src.at[:, hidden_cols(target)], dst.at[at.y, at.z], ex_send.at[k, d], ex_recv.at[k, d], at.at_y(target)
        )

    def z_start(k, src, dst):
        for d in range(1, at.z_n):
            z_copy(k, src, dst, d).start()
        dst[at.y, at.z] = src[:, feature_cols(at.z)]

    def y_start(k, src, dst):
        for d in range(1, at.y_n):
            y_copy(k, src, dst, d).start()
        dst[at.y, at.z] = src[:, hidden_cols(at.y)]

    def z_wait(k, dst):
        for d in range(1, at.z_n):
            spot = dst.at[at.y, at.step_z(-d)]
            remote(spot, spot, ex_send.at[k, d], ex_recv.at[k, d], at.at_z(at.step_z(d))).wait_recv()

    def y_wait(k, dst):
        for d in range(1, at.y_n):
            spot = dst.at[at.step_y(-d), at.z]
            remote(spot, spot, ex_send.at[k, d], ex_recv.at[k, d], at.at_y(at.step_y(d))).wait_recv()

    def ex_wait_send(k, copy, src, dst, n):
        for d in range(1, n):
            copy(k, src, dst, d).wait_send()

    def row_rings(ref, first):
        part = at.z_n // 2
        return [
            Ring(*y_ring, lambda y, c=c: ref.at[y, pl.ds(c * part, part)], at.at_y, sems, first + c, c) for c in range(2)
        ]

    def column_rings(ref, first):
        part = at.y_n // 2
        return [
            Ring(*z_ring, lambda z, c=c: ref.at[pl.ds(c * part, part), z], at.at_z, sems, first + c, c) for c in range(2)
        ]

    normed_rings = row_rings(normed_all, index)
    g_rings = row_rings(g_all, index + 2)
    act_rings = column_rings(act_all, index + 4)
    pg_rings = column_rings(pg_all, index + 6)

    def early():
        y_start(2, act, act_all)
        z_start(0, normed, normed_all)
        for ring in weight_rings:
            ring.wait_send()
        y_wait(2, act_all)
        z_wait(0, normed_all)
        run_rings(act_rings + normed_rings)
        for ring in act_rings + normed_rings:
            ring.wait_send()
        ex_wait_send(0, z_copy, normed, normed_all, at.z_n)
        ex_wait_send(2, y_copy, act, act_all, at.y_n)

    @pl.when(not_first)
    def _():
        for j in range(2):
            fwd_copy(j).wait_recv()

    @pl.when(section == 0)
    def _():
        load_emb.wait()

    values = x_in[...].astype(F32)
    centered = values - jnp.mean(values, axis=-1, keepdims=True)
    inverse = lax.rsqrt(jnp.mean(centered * centered, axis=-1, keepdims=True) + epsilon)
    unit_values = centered * inverse
    normed[...] = (unit_values * gain_ref[...] + bias_ref[...]).astype(BF16)
    unit[...] = unit_values
    inv[...] = jnp.broadcast_to(inverse, inv.shape)

    def up_half(h, _):
        pre = jnp.dot(normed[...], up_weights(h), preferred_element_type=F32) + bias_all[h, 0:1, :]
        slope[:, hidden_half(h)] = pre
        act[:, hidden_half(h)] = gelu_value(pre).astype(BF16)
        return 0

    lax.fori_loop(0, 2, up_half, 0)

    def down_half(j, _):
        cols = columns(j)
        total = outer_t(act[:, :half], quarter(down_all, 0, j)) + outer_t(act[:, half:], quarter(down_all, 1, j))
        output = (x_in[:, cols].astype(F32) + total + bdown_ref[:, cols]).astype(BF16)
        out_rows[:, cols] = output
        code_f[:, cols] = coded(output, fst[sid, :, cols], bound_f[:, cols])

        @pl.when(not_last)
        def _():
            fwd_copy(j).start()

        return 0

    lax.fori_loop(0, 2, down_half, 0)
    out_keep = pltpu.make_async_copy(out_rows, out_ref.at[mine], load_sem.at[6])
    out_keep.start()
    out_copy = remote(out_rows, out_ref.at[mine], peer_send.at[0], peer_recv.at[0], peer)
    out_copy.start()

    def slope_half(h, _):
        slope[:, hidden_half(h)] = gelu_slope(slope[:, hidden_half(h)])
        return 0

    lax.fori_loop(0, 2, slope_half, 0)

    @pl.when(early_first)
    def _():
        early()

    @pl.when(not_last)
    def _():
        for j in range(2):
            bwd_copy(j).wait_recv()

    @pl.when(jnp.logical_not(not_last))
    def _():
        load_cot.wait()

    def up_grad_half(h, _):
        act_grad = jnp.dot(g_in[...], down_weights(h), preferred_element_type=F32)
        pre_grad[:, hidden_half(h)] = (act_grad * slope[:, hidden_half(h)]).astype(BF16)
        return 0

    lax.fori_loop(0, 2, up_grad_half, 0)
    y_start(3, pre_grad, pg_all)
    z_start(1, g_in, g_all)

    def norm_grad_half(j, _):
        cols = columns(j)
        total = outer_t(pre_grad[:, :half], quarter(up_all, 0, j)) + outer_t(pre_grad[:, half:], quarter(up_all, 1, j))
        scaled[:, cols] = total * gain_ref[:, cols]
        return 0

    lax.fori_loop(0, 2, norm_grad_half, 0)
    scaled_values = scaled[...]
    unit_values = unit[...]
    first_mean = jnp.mean(scaled_values, axis=-1, keepdims=True)
    second_mean = jnp.mean(scaled_values * unit_values, axis=-1, keepdims=True)

    for j in range(2):
        cols = pl.ds(j * wide, wide)
        inner_part = scaled[:, cols] - first_mean - unit[:, cols] * second_mean
        input_grad = (g_in[:, cols].astype(F32) + inv[:, 0:1] * inner_part).astype(BF16)
        ig_rows[:, cols] = input_grad
        code_b[:, cols] = coded(input_grad, bst[sid, :, cols], bound_b[:, cols])

        @pl.when(not_first)
        def _():
            bwd_copy(j).start()

    ig_keep = pltpu.make_async_copy(ig_rows, ig_ref.at[mine], load_sem.at[7])
    ig_keep.start()
    ig_copy = remote(ig_rows, ig_ref.at[mine], peer_send.at[1], peer_recv.at[1], peer)
    ig_copy.start()

    @pl.when(jnp.logical_not(early_first))
    def _():
        early()

    up_block[...] = jnp.zeros_like(up_block)
    down_block[...] = jnp.zeros_like(down_block)
    y_wait(3, pg_all)
    z_wait(1, g_all)

    def add_column(z):
        left = normed_all[:, z].reshape(at.y_n * rows, features)
        up_block[...] += inner(left, pg_all[:, z].reshape(at.y_n * rows, hidden))

    def add_row(y):
        left = g_all[y].reshape(at.z_n * rows, features)
        down_block[...] += inner(left, act_all[y].reshape(at.z_n * rows, hidden))

    def add_round(r):
        for n, step, add in ((at.z_n, at.step_z, add_column), (at.y_n, at.step_y, add_row)):
            if r + 1 < n // 2:
                lax.fori_loop(0, 2, lambda i, _, step=step, add=add: (add(step((2 * i - 1) * (r + 1))), 0)[1], 0)
            elif r + 1 == n // 2:
                add(step(r + 1))
            if r == 0:
                add(step(0))

    run_rings(pg_rings + g_rings, add_round)

    out_cols = pl.ds(pl.multiple_of(at.hi * hidden, hidden), hidden)
    outs = ((0, up_block, up_out), (1, down_block, down_out))

    def grad_copy(k, block, out, i):
        return remote(
            block.at[pl.ds(i * shard, shard)],
            out.at[:, out_cols],
            out_send.at[k, i],
            out_recv.at[k, at.hi],
            {"dp": at.z * at.y_hi_n + i},
        )

    def grad_keep(k, block, out, i):
        return pltpu.make_async_copy(block.at[pl.ds(i * shard, shard)], out.at[:, out_cols], out_send.at[k, i])

    for i in range(at.y_hi_n):
        own = at.z * at.y_hi_n + i == at.dp

        @pl.when(jnp.logical_not(own))
        def _():
            for k, block, out in outs:
                grad_copy(k, block, out, i).start()

        @pl.when(own)
        def _():
            for k, block, out in outs:
                grad_keep(k, block, out, i).start()

    @pl.when(not_last)
    def _():
        for j in range(2):
            fwd_copy(j).wait_send()

    @pl.when(not_first)
    def _():
        for j in range(2):
            bwd_copy(j).wait_send()

    ex_wait_send(1, z_copy, g_in, g_all, at.z_n)
    ex_wait_send(3, y_copy, pre_grad, pg_all, at.y_n)
    for ring in pg_rings + g_rings:
        ring.wait_send()
    remote(out_rows, out_ref.at[other], peer_send.at[0], peer_recv.at[0], peer).wait_recv()
    remote(ig_rows, ig_ref.at[other], peer_send.at[1], peer_recv.at[1], peer).wait_recv()
    out_copy.wait_send()
    ig_copy.wait_send()
    out_keep.wait()
    ig_keep.wait()

    for i in range(at.y_hi_n):

        @pl.when(i * at.z_n + owner_z != at.dp)
        def _():
            for k, block, out in outs:
                spot = out.at[:, pl.ds(i * hidden, hidden)]
                remote(spot, spot, out_send.at[k, 0], out_recv.at[k, i], {"dp": at.z * at.y_hi_n + i}).wait_recv()

    for i in range(at.y_hi_n):
        own = at.z * at.y_hi_n + i == at.dp

        @pl.when(jnp.logical_not(own))
        def _():
            for k, block, out in outs:
                grad_copy(k, block, out, i).wait_send()

        @pl.when(own)
        def _():
            for k, block, out in outs:
                grad_keep(k, block, out, i).wait()


def keep_kernel(*refs):
    count = len(refs) // 2
    sems = refs[-1]
    copies = [pltpu.make_async_copy(refs[i], refs[count + i], sems.at[i]) for i in range(count)]
    for copy in copies:
        copy.start()
    for copy in copies:
        copy.wait()


def vmem(count):
    return [pl.BlockSpec(memory_space=pltpu.VMEM)] * count


def anywhere(count):
    return [pl.BlockSpec(memory_space=pl.ANY)] * count


def per_device(
    n_sections,
    n_dp,
    y_hi,
    embeddings,
    cotangent,
    w_up,
    w_down,
    b_up,
    b_down,
    ln_gain,
    ln_bias,
    fwd_store,
    bwd_store,
    sample_ids,
    fwd_scales,
    bwd_scales,
):
    z_n = n_dp // y_hi
    y_n = y_hi * Y_LO
    shard, half = w_up.shape[1:]
    width = embeddings.shape[1]
    rows = embeddings.shape[0] // Y_LO
    hidden_all = Y_LO * half
    features = width // z_n
    hidden = hidden_all // y_n
    stored = fwd_store.shape[1]
    dma = pltpu.SemaphoreType.DMA
    rounds = max(y_n, z_n) // 2
    n_rings = 2 + y_n + z_n + 8
    peers = max(y_n, z_n)
    whole = pltpu.VMEM((Y_LO, y_hi, z_n, shard, half), BF16)
    narrow = pltpu.VMEM((rows, width), BF16)
    wide = pltpu.VMEM((rows, width), F32)
    outs = (
        jax.ShapeDtypeStruct(embeddings.shape, BF16),
        jax.ShapeDtypeStruct(embeddings.shape, BF16),
        jax.ShapeDtypeStruct((shard, half), F32),
        jax.ShapeDtypeStruct((shard, half), F32),
    )
    results = pl.pallas_call(
        functools.partial(layer_kernel, n_sections, n_dp, y_hi),
        out_shape=outs,
        in_specs=[pl.BlockSpec(memory_space=pltpu.SMEM)] + anywhere(4) + vmem(4) + anywhere(2) + vmem(2),
        out_specs=tuple(anywhere(4)),
        scratch_shapes=[
            whole,
            whole,
            pltpu.VMEM((Y_LO, 8, half), F32),
            narrow,
            narrow,
            pltpu.VMEM((stored, rows, width), BF16),
            pltpu.VMEM((stored, rows, width), BF16),
            narrow,
            pltpu.VMEM((rows, hidden_all), BF16),
            pltpu.VMEM((rows, hidden_all), BF16),
            narrow,
            narrow,
            narrow,
            narrow,
            wide,
            wide,
            pltpu.VMEM((rows, hidden_all), F32),
            wide,
            pltpu.VMEM((rows, 128), F32),
            wide,
            pltpu.VMEM((y_n, z_n, rows, features), BF16),
            pltpu.VMEM((y_n, z_n, rows, hidden), BF16),
            pltpu.VMEM((y_n, z_n, rows, hidden), BF16),
            pltpu.VMEM((y_n, z_n, rows, features), BF16),
            pltpu.VMEM((features, hidden), F32),
            pltpu.VMEM((features, hidden), F32),
            dma((8,)),
            dma((2,)),
            dma((2, 2)),
            dma((2, 2)),
            dma((2,)),
            dma((2,)),
            dma((n_rings, 2, rounds)),
            dma((n_rings, 2, rounds)),
            dma((4, peers)),
            dma((4, peers)),
            dma((2, y_hi)),
            dma((2, y_hi)),
        ],
        compiler_params=pltpu.CompilerParams(
            collective_id=0, has_side_effects=True, vmem_limit_bytes=56 * 1024 * 1024
        ),
    )(
        sample_ids,
        embeddings,
        cotangent,
        w_up[0],
        w_down[0].T,
        b_up,
        b_down,
        ln_gain,
        ln_bias,
        fwd_store[0],
        bwd_store[0],
        fwd_scales[0].T,
        bwd_scales[0].T,
    )
    kept = pl.pallas_call(
        keep_kernel,
        out_shape=outs,
        in_specs=anywhere(4),
        out_specs=tuple(anywhere(4)),
        scratch_shapes=[dma((4,))],
    )(*results)
    return tuple(array[None] for array in kept)


def solution(mesh, y_hi=Y_HI):
    return jax.shard_map(
        functools.partial(per_device, mesh.shape["section"], mesh.shape["dp"], y_hi),
        mesh=mesh,
        in_specs=(
            P("dp", None),
            P("dp", None),
            P("section", "dp", "tensor"),
            P("section", "tensor", "dp"),
            P("section", "tensor"),
            P("section", None),
            P("section", None),
            P("section", None),
            P("section", "dp", None, None),
            P("section", "dp", None, None),
            P("dp"),
            P("section", "dp", None),
            P("section", "dp", None),
        ),
        out_specs=(
            P("section", "dp", None),
            P("section", "dp", None),
            P("section", "dp", "tensor"),
            P("section", "dp", "tensor"),
        ),
        check_vma=False,
    )
```

```python
import functools

import jax
import jax.numpy as jnp
from jax import lax
from jax.experimental import pallas as pl
from jax.experimental.pallas import tpu as pltpu
from jax.sharding import PartitionSpec as P

MESH = pl.DeviceIdType.MESH
BF16 = jnp.bfloat16
F32 = jnp.float32
Y_LO = 2
Y_HI = 4

root_half = 0.7071067811865476
density = 0.3989422804014327
epsilon = 1e-05


class Place:
    def __init__(self, n_dp, y_hi=Y_HI):
        self.y_hi_n = y_hi
        self.z_n = n_dp // y_hi
        self.y_n = y_hi * Y_LO
        self.dp = lax.axis_index("dp")
        self.lo = lax.axis_index("tensor")
        self.hi = self.dp // self.z_n
        self.z = self.dp % self.z_n
        self.y = self.hi * Y_LO + self.lo

    def at_y(self, y):
        return {"dp": (y // Y_LO) * self.z_n + self.z, "tensor": y % Y_LO}

    def at_z(self, z):
        return {"dp": self.hi * self.z_n + z, "tensor": self.lo}

    def step_y(self, d):
        return (self.y + d + self.y_n) % self.y_n

    def step_z(self, d):
        return (self.z + d + self.z_n) % self.z_n


def signal(barrier, device_id):
    pl.semaphore_signal(barrier, inc=1, device_id=device_id, device_id_type=MESH)


def remote(src, dst, send_sem, recv_sem, device_id):
    return pltpu.make_async_remote_copy(
        src_ref=src, dst_ref=dst, send_sem=send_sem, recv_sem=recv_sem, device_id=device_id, device_id_type=MESH
    )


class Ring:
    def __init__(self, n, step, slot, device, sems, index, last_way):
        self.step, self.slot, self.device = step, slot, device
        self.send_sem, self.recv_sem, self.index = sems[0], sems[1], index
        self.rounds = n // 2
        self.last_way = last_way

    def ways(self, r):
        return (self.last_way,) if r == self.rounds - 1 else (0, 1)

    def copy(self, way, r, received=False):
        sign = 1 - 2 * way
        block = self.slot(self.step(-sign * (r + 1 if received else r)))
        spot = (self.index, way, r)
        return remote(block, block, self.send_sem.at[spot], self.recv_sem.at[spot], self.device(self.step(sign)))

    def start(self, r):
        for way in self.ways(r):
            self.copy(way, r).start()

    def wait_recv(self, r):
        for way in self.ways(r):
            self.copy(way, r, True).wait_recv()

    def wait_send(self):
        for r in range(self.rounds):
            for way in self.ways(r):
                self.copy(way, r).wait_send()


class Spread:
    def __init__(self, n, step, part, slot, device, sems, index):
        self.step, self.part, self.slot, self.device = step, part, slot, device
        self.send_sem, self.recv_sem, self.index = sems[0], sems[1], index
        self.rounds = n // 2

    def ways(self, r):
        return (0,) if r == self.rounds - 1 else (0, 1)

    def copy(self, way, r, received=False):
        sign = 1 - 2 * way
        spot = (self.index, way, r)
        target = self.step(sign * (r + 1))
        block = self.slot(self.step(-sign * (r + 1) if received else 0))
        source = block if received else self.part(target)
        return remote(source, block, self.send_sem.at[spot], self.recv_sem.at[spot], self.device(target))

    wait_send = Ring.wait_send


def start_spreads(pairs):
    for r in range(max(pair[1].rounds for pair in pairs)):
        for pair in pairs:
            if r < pair[1].rounds:
                for way in pair[1].ways(r):
                    pair[1].copy(way, r).start()


def run_gathers(pairs, lag=1.0):
    free, events, count, missing, brought = {}, [], [0], {}, {}

    def push(ready, axis, ring, way, r, pair, size=1.0):
        begin = max(ready, free.get((axis, way), 0.0))
        free[axis, way] = begin + size
        count[0] += 1
        events.append((begin + size + lag, count[0], ring, way, r, pair))

    def go(ready, axis, ring, way, r, pair):
        push(ready, axis, ring, way, r, pair)
        ring.copy(way, r).start()

    def begin_chunk(ready, pair, d):
        for way in pair[3][d].ways(0):
            go(ready, pair[2], pair[3][d], way, 0, pair)

    def arrived(pair, n, d):
        key = (id(pair), d if d * 2 > -n else d + n)
        missing[key] = missing.get(key, len(pair[3])) - 1
        if missing[key] == 0 and pair[4] is not None:
            pair[4](d)

    for pair in pairs:
        spread = isinstance(pair[1], Spread)
        for r in range(pair[1].rounds if spread else 1):
            for way in pair[1].ways(r):
                if spread:
                    push(0.0, pair[0], pair[1], way, r, pair, r + 1.0)
                else:
                    go(0.0, pair[0], pair[1], way, r, pair)
    for pair in pairs:
        begin_chunk(0.0, pair, 0)
        arrived(pair, 2 * pair[3][0].rounds, 0)
    while events:
        event = min(events, key=lambda e: e[:2])
        events.remove(event)
        now, _, ring, way, r, pair = event
        ring.copy(way, r, True).wait_recv()
        d = -(r + 1) if way == 0 else r + 1
        first = ring is pair[1]
        if not (first and isinstance(ring, Spread)) and r + 1 < ring.rounds and way in ring.ways(r + 1):
            go(now, pair[0] if first else pair[2], ring, way, r + 1, pair)
        if first:
            begin_chunk(now, pair, d)
            arrived(pair, 2 * pair[3][0].rounds, 0)
        else:
            arrived(pair, 2 * ring.rounds, d)


def gelu_value(pre_gelu):
    return pre_gelu * 0.5 * (1.0 + lax.erf(pre_gelu * root_half))


def gelu_slope(pre_gelu):
    return (
        0.5 * (1.0 + lax.erf(pre_gelu * root_half))
        + pre_gelu * jnp.exp(-0.5 * pre_gelu * pre_gelu) * density
    )


def outer_t(left, right):
    return lax.dot_general(left, right, (((1,), (1,)), ((), ())), preferred_element_type=F32)


def inner(left, right):
    return lax.dot_general(left, right, (((0,), (0,)), ((), ())), preferred_element_type=F32)


def coded(values, base, bound):
    base = base.astype(F32)
    return (base + jnp.clip(values.astype(F32) - base, -bound, bound)).astype(BF16)


def layer_kernel(
    n_sections,
    n_dp,
    y_hi,
    sid_ref,
    emb_ref,
    cot_ref,
    up_ref,
    down_ref,
    bup_ref,
    bdown_ref,
    gain_ref,
    bias_ref,
    fst_ref,
    bst_ref,
    fsc_ref,
    bsc_ref,
    out_ref,
    ig_ref,
    up_out,
    down_out,
    up_all,
    down_all,
    bias_all,
    x_in,
    g_in,
    fst,
    bst,
    normed,
    act,
    pre_grad,
    out_rows,
    ig_rows,
    code_f,
    code_b,
    bound_f,
    bound_b,
    slope,
    unit,
    inv,
    scaled,
    normed_all,
    act_all,
    pg_all,
    g_all,
    up_block,
    down_block,
    load_sem,
    bias_sem,
    hop_send,
    hop_recv,
    peer_send,
    peer_recv,
    ring_send,
    ring_recv,
    out_send,
    out_recv,
):
    at = Place(n_dp, y_hi)
    section = lax.axis_index("section")
    rows, width = x_in.shape
    half = up_all.shape[2]
    features = normed_all.shape[3]
    hidden = act_all.shape[3]
    shard = up_ref.shape[0]
    wide = width // 2
    sems = (ring_send, ring_recv)
    mine = pl.ds(pl.multiple_of(at.lo * rows, rows), rows)
    other = pl.ds(pl.multiple_of((1 - at.lo) * rows, rows), rows)
    not_first = section > 0
    not_last = section < n_sections - 1
    early_first = section < n_sections // 2
    after = {"section": jnp.minimum(section + 1, n_sections - 1)}
    before = {"section": jnp.maximum(section - 1, 0)}
    peer = {"tensor": 1 - at.lo}
    owner_z = at.dp // at.y_hi_n

    barrier = pltpu.get_barrier_semaphore()
    for d in range(1, at.y_n):
        signal(barrier, at.at_y(at.step_y(d)))
    for d in range(1, at.z_n):
        signal(barrier, at.at_z(at.step_z(d)))
    for i in range(at.y_hi_n):
        source = i * at.z_n + owner_z

        @pl.when(source != at.dp)
        def _():
            signal(barrier, {"dp": source})

    @pl.when(not_first)
    def _():
        signal(barrier, before)

    @pl.when(not_last)
    def _():
        signal(barrier, after)

    own_rows = pl.ds(pl.multiple_of(at.dp * shard, shard), shard)
    own_up = pltpu.make_async_copy(up_ref, up_all.at[at.lo, own_rows], load_sem.at[0])
    own_down = pltpu.make_async_copy(down_ref, down_all.at[at.lo, own_rows], load_sem.at[1])
    load_fst = pltpu.make_async_copy(fst_ref.at[:, mine], fst, load_sem.at[2])
    load_bst = pltpu.make_async_copy(bst_ref.at[:, mine], bst, load_sem.at[3])
    load_emb = pltpu.make_async_copy(emb_ref.at[mine], x_in, load_sem.at[4])
    load_cot = pltpu.make_async_copy(cot_ref.at[mine], g_in, load_sem.at[5])
    own_up.start()
    own_down.start()
    load_fst.start()
    load_bst.start()

    @pl.when(section == 0)
    def _():
        load_emb.start()

    @pl.when(jnp.logical_not(not_last))
    def _():
        load_cot.start()

    bias_all[at.lo] = jnp.broadcast_to(bup_ref[...], bias_all.shape[1:])
    sends_self = jnp.int32(0)
    for i in range(at.y_hi_n):
        sends_self = sends_self + (at.z * at.y_hi_n + i == at.dp).astype(jnp.int32)
    sections_near = not_first.astype(jnp.int32) + not_last.astype(jnp.int32)
    own_up.wait()
    own_down.wait()
    pl.semaphore_wait(barrier, at.y_n + at.z_n - 2 + at.y_hi_n - sends_self + sections_near)

    bias_copy = remote(bias_all.at[at.lo], bias_all.at[at.lo], bias_sem.at[0], bias_sem.at[1], peer)
    bias_copy.start()

    def shard_rows(y, z):
        return pl.ds(pl.multiple_of(((y // Y_LO) * at.z_n + z) * shard, shard), shard)

    def up_slot(y, z):
        return up_all.at[y % Y_LO, shard_rows(y, z)]

    def down_slot(y, z):
        return down_all.at[y % Y_LO, shard_rows(y, z)]

    def fixed(slot, axis, step, d):
        there = step(d)
        return (lambda z: slot(there, z)) if axis == "y" else (lambda y: slot(y, there))

    y_ring = (at.y_n, at.step_y)
    z_ring = (at.z_n, at.step_z)
    up_first = Ring(*y_ring, fixed(up_slot, "z", at.step_z, 0), at.at_y, sems, 0, 0)
    down_first = Ring(*z_ring, fixed(down_slot, "y", at.step_y, 0), at.at_z, sems, 1, 1)
    up_then, down_then = {}, {}
    index = 2
    for d in range(-(at.y_n // 2), at.y_n // 2):
        up_then[d] = Ring(*z_ring, fixed(up_slot, "y", at.step_y, d), at.at_z, sems, index, index % 2)
        index += 1
    for d in range(-(at.z_n // 2), at.z_n // 2):
        down_then[d] = Ring(*y_ring, fixed(down_slot, "z", at.step_z, d), at.at_y, sems, index, index % 2)
        index += 1
    if down_first.last_way == 1:
        down_then[at.z_n // 2] = down_then.pop(-(at.z_n // 2))
    weight_rings = [up_first, down_first, *up_then.values(), *down_then.values()]
    run_gathers((("y", up_first, "z", up_then, None), ("z", down_first, "y", down_then, None)))

    scale_f = jnp.transpose(fsc_ref[...].astype(F32))
    scale_b = jnp.transpose(bsc_ref[...].astype(F32))
    low = at.lo == 0
    scale_f = 0.25 * jnp.where(low, scale_f[:rows], scale_f[rows:])
    scale_b = 0.25 * jnp.where(low, scale_b[:rows], scale_b[rows:])
    for b in range(fsc_ref.shape[0]):
        block = width // fsc_ref.shape[0]
        cols = pl.ds(b * block, block)
        bound_f[:, cols] = jnp.broadcast_to(scale_f[:, b : b + 1], (rows, block))
        bound_b[:, cols] = jnp.broadcast_to(scale_b[:, b : b + 1], (rows, block))
    remote(bias_all.at[1 - at.lo], bias_all.at[1 - at.lo], bias_sem.at[0], bias_sem.at[1], peer).wait_recv()
    bias_copy.wait_send()
    load_fst.wait()
    load_bst.wait()
    sid = sid_ref[0]

    def columns(j):
        return pl.ds(pl.multiple_of(j * wide, wide), wide)

    def fwd_copy(j):
        return remote(code_f.at[:, columns(j)], x_in.at[:, columns(j)], hop_send.at[0, j], hop_recv.at[0, j], after)

    def bwd_copy(j):
        return remote(code_b.at[:, columns(j)], g_in.at[:, columns(j)], hop_send.at[1, j], hop_recv.at[1, j], before)

    def hidden_half(h):
        return pl.ds(pl.multiple_of(h * half, half), half)

    def feature_cols(z):
        return pl.ds(pl.multiple_of(z * features, features), features)

    def hidden_cols(y):
        spot = (y % Y_LO) * at.y_hi_n + y // Y_LO
        return pl.ds(pl.multiple_of(spot * hidden, hidden), hidden)

    def exchange(src, dst, along_z, index, done=None):
        if along_z:
            spread = Spread(*z_ring, lambda z: src.at[:, feature_cols(z)], lambda z: dst.at[at.y, z], at.at_z, sems, index)
            there, ring, device = at.step_z, y_ring, at.at_y
        else:
            spread = Spread(*y_ring, lambda y: src.at[:, hidden_cols(y)], lambda y: dst.at[y, at.z], at.at_y, sems, index)
            there, ring, device = at.step_y, z_ring, at.at_z
        n = z_ring[0] if along_z else y_ring[0]
        rings = {}
        for d in range(1 - n // 2, n // 2 + 1):
            index += 1

            def slot(i, d=d):
                return dst.at[i, there(d)] if along_z else dst.at[there(d), i]

            rings[d if d < n // 2 else -d] = Ring(*ring, slot, device, sems, index, index % 2)
        axes = ("z", "y") if along_z else ("y", "z")
        return (axes[0], spread, axes[1], rings, done)

    def keep_own(src, dst, along_z):
        dst[at.y, at.z] = src[:, feature_cols(at.z)] if along_z else src[:, hidden_cols(at.y)]

    def add_column(d):
        z = at.step_z(d)
        left = normed_all[:, z].reshape(at.y_n * rows, features)
        up_block[...] += inner(left, pg_all[:, z].reshape(at.y_n * rows, hidden))

    def add_row(d):
        y = at.step_y(d)
        left = g_all[y].reshape(at.z_n * rows, features)
        down_block[...] += inner(left, act_all[y].reshape(at.z_n * rows, hidden))

    act_pair = exchange(act, act_all, False, index)
    normed_pair = exchange(normed, normed_all, True, index + 1 + at.y_n)
    pg_pair = exchange(pre_grad, pg_all, False, index + 2 + at.y_n + at.z_n, add_column)
    g_pair = exchange(g_in, g_all, True, index + 3 + 2 * at.y_n + at.z_n, add_row)
    early_pairs, late_pairs = (act_pair, normed_pair), (pg_pair, g_pair)

    def wait_sends(pairs):
        for pair in pairs:
            for ring in (pair[1], *pair[3].values()):
                ring.wait_send()

    def early():
        start_spreads(early_pairs)
        keep_own(act, act_all, False)
        keep_own(normed, normed_all, True)
        for ring in weight_rings:
            ring.wait_send()
        run_gathers(early_pairs)
        wait_sends(early_pairs)

    @pl.when(not_first)
    def _():
        for j in range(2):
            fwd_copy(j).wait_recv()

    @pl.when(section == 0)
    def _():
        load_emb.wait()

    values = x_in[...].astype(F32)
    centered = values - jnp.mean(values, axis=-1, keepdims=True)
    inverse = lax.rsqrt(jnp.mean(centered * centered, axis=-1, keepdims=True) + epsilon)
    unit_values = centered * inverse
    normed[...] = (unit_values * gain_ref[...] + bias_ref[...]).astype(BF16)
    unit[...] = unit_values
    inv[...] = jnp.broadcast_to(inverse, inv.shape)

    def up_half(h, _):
        pre = jnp.dot(normed[...], up_all[h], preferred_element_type=F32) + bias_all[h, 0:1, :]
        slope[:, hidden_half(h)] = pre
        act[:, hidden_half(h)] = gelu_value(pre).astype(BF16)
        return 0

    lax.fori_loop(0, 2, up_half, 0)

    def down_half(j, _):
        cols = columns(j)
        total = outer_t(act[:, :half], down_all[0, cols, :]) + outer_t(act[:, half:], down_all[1, cols, :])
        output = (x_in[:, cols].astype(F32) + total + bdown_ref[:, cols]).astype(BF16)
        out_rows[:, cols] = output
        code_f[:, cols] = coded(output, fst[sid, :, cols], bound_f[:, cols])

        @pl.when(not_last)
        def _():
            fwd_copy(j).start()

        return 0

    lax.fori_loop(0, 2, down_half, 0)
    out_keep = pltpu.make_async_copy(out_rows, out_ref.at[mine], load_sem.at[6])
    out_keep.start()
    out_copy = remote(out_rows, out_ref.at[mine], peer_send.at[0], peer_recv.at[0], peer)
    out_copy.start()

    def slope_half(h, _):
        slope[:, hidden_half(h)] = gelu_slope(slope[:, hidden_half(h)])
        return 0

    lax.fori_loop(0, 2, slope_half, 0)

    @pl.when(early_first)
    def _():
        early()

    @pl.when(not_last)
    def _():
        for j in range(2):
            bwd_copy(j).wait_recv()

    @pl.when(jnp.logical_not(not_last))
    def _():
        load_cot.wait()

    def up_grad_half(h, _):
        act_grad = jnp.dot(g_in[...], down_all[h], preferred_element_type=F32)
        pre_grad[:, hidden_half(h)] = (act_grad * slope[:, hidden_half(h)]).astype(BF16)
        return 0

    lax.fori_loop(0, 2, up_grad_half, 0)
    start_spreads(late_pairs)
    keep_own(pre_grad, pg_all, False)
    keep_own(g_in, g_all, True)

    def norm_grad_half(j, _):
        cols = columns(j)
        total = outer_t(pre_grad[:, :half], up_all[0, cols, :]) + outer_t(pre_grad[:, half:], up_all[1, cols, :])
        scaled[:, cols] = total * gain_ref[:, cols]
        return 0

    lax.fori_loop(0, 2, norm_grad_half, 0)
    scaled_values = scaled[...]
    unit_values = unit[...]
    first_mean = jnp.mean(scaled_values, axis=-1, keepdims=True)
    second_mean = jnp.mean(scaled_values * unit_values, axis=-1, keepdims=True)

    for j in range(2):
        cols = pl.ds(j * wide, wide)
        inner_part = scaled[:, cols] - first_mean - unit[:, cols] * second_mean
        input_grad = (g_in[:, cols].astype(F32) + inv[:, 0:1] * inner_part).astype(BF16)
        ig_rows[:, cols] = input_grad
        code_b[:, cols] = coded(input_grad, bst[sid, :, cols], bound_b[:, cols])

        @pl.when(not_first)
        def _():
            bwd_copy(j).start()

    ig_keep = pltpu.make_async_copy(ig_rows, ig_ref.at[mine], load_sem.at[7])
    ig_keep.start()
    ig_copy = remote(ig_rows, ig_ref.at[mine], peer_send.at[1], peer_recv.at[1], peer)
    ig_copy.start()

    @pl.when(jnp.logical_not(early_first))
    def _():
        early()

    up_block[...] = jnp.zeros_like(up_block)
    down_block[...] = jnp.zeros_like(down_block)
    run_gathers(late_pairs)

    out_cols = pl.ds(pl.multiple_of(at.hi * hidden, hidden), hidden)
    outs = ((0, up_block, up_out), (1, down_block, down_out))

    def grad_copy(k, block, out, i):
        return remote(
            block.at[pl.ds(i * shard, shard)],
            out.at[:, out_cols],
            out_send.at[k, i],
            out_recv.at[k, at.hi],
            {"dp": at.z * at.y_hi_n + i},
        )

    def grad_keep(k, block, out, i):
        return pltpu.make_async_copy(block.at[pl.ds(i * shard, shard)], out.at[:, out_cols], out_send.at[k, i])

    for i in range(at.y_hi_n):
        own = at.z * at.y_hi_n + i == at.dp

        @pl.when(jnp.logical_not(own))
        def _():
            for k, block, out in outs:
                grad_copy(k, block, out, i).start()

        @pl.when(own)
        def _():
            for k, block, out in outs:
                grad_keep(k, block, out, i).start()

    @pl.when(not_last)
    def _():
        for j in range(2):
            fwd_copy(j).wait_send()

    @pl.when(not_first)
    def _():
        for j in range(2):
            bwd_copy(j).wait_send()

    wait_sends(late_pairs)
    remote(out_rows, out_ref.at[other], peer_send.at[0], peer_recv.at[0], peer).wait_recv()
    remote(ig_rows, ig_ref.at[other], peer_send.at[1], peer_recv.at[1], peer).wait_recv()
    out_copy.wait_send()
    ig_copy.wait_send()
    out_keep.wait()
    ig_keep.wait()

    for i in range(at.y_hi_n):

        @pl.when(i * at.z_n + owner_z != at.dp)
        def _():
            for k, block, out in outs:
                spot = out.at[:, pl.ds(i * hidden, hidden)]
                remote(spot, spot, out_send.at[k, 0], out_recv.at[k, i], {"dp": at.z * at.y_hi_n + i}).wait_recv()

    for i in range(at.y_hi_n):
        own = at.z * at.y_hi_n + i == at.dp

        @pl.when(jnp.logical_not(own))
        def _():
            for k, block, out in outs:
                grad_copy(k, block, out, i).wait_send()

        @pl.when(own)
        def _():
            for k, block, out in outs:
                grad_keep(k, block, out, i).wait()


def keep_kernel(*refs):
    count = len(refs) // 2
    for source, target in zip(refs[:count], refs[count:]):
        target[...] = source[...]


def vmem(count):
    return [pl.BlockSpec(memory_space=pltpu.VMEM)] * count


def anywhere(count):
    return [pl.BlockSpec(memory_space=pl.ANY)] * count


def per_device(
    n_sections,
    n_dp,
    y_hi,
    embeddings,
    cotangent,
    w_up,
    w_down,
    b_up,
    b_down,
    ln_gain,
    ln_bias,
    fwd_store,
    bwd_store,
    sample_ids,
    fwd_scales,
    bwd_scales,
):
    z_n = n_dp // y_hi
    y_n = y_hi * Y_LO
    shard, half = w_up.shape[1:]
    width = embeddings.shape[1]
    rows = embeddings.shape[0] // Y_LO
    hidden_all = Y_LO * half
    features = width // z_n
    hidden = hidden_all // y_n
    stored = fwd_store.shape[1]
    dma = pltpu.SemaphoreType.DMA
    rounds = max(y_n, z_n) // 2
    n_rings = 6 + 3 * (y_n + z_n)
    whole = pltpu.VMEM((Y_LO, width, half), BF16)
    narrow = pltpu.VMEM((rows, width), BF16)
    wide = pltpu.VMEM((rows, width), F32)
    outs = (
        jax.ShapeDtypeStruct(embeddings.shape, BF16),
        jax.ShapeDtypeStruct(embeddings.shape, BF16),
        jax.ShapeDtypeStruct((shard, half), F32),
        jax.ShapeDtypeStruct((shard, half), F32),
    )
    results = pl.pallas_call(
        functools.partial(layer_kernel, n_sections, n_dp, y_hi),
        out_shape=outs,
        in_specs=[pl.BlockSpec(memory_space=pltpu.SMEM)] + anywhere(4) + vmem(4) + anywhere(2) + vmem(2),
        out_specs=tuple(anywhere(4)),
        scratch_shapes=[
            whole,
            whole,
            pltpu.VMEM((Y_LO, 8, half), F32),
            narrow,
            narrow,
            pltpu.VMEM((stored, rows, width), BF16),
            pltpu.VMEM((stored, rows, width), BF16),
            narrow,
            pltpu.VMEM((rows, hidden_all), BF16),
            pltpu.VMEM((rows, hidden_all), BF16),
            narrow,
            narrow,
            narrow,
            narrow,
            wide,
            wide,
            pltpu.VMEM((rows, hidden_all), F32),
            wide,
            pltpu.VMEM((rows, 128), F32),
            wide,
            pltpu.VMEM((y_n, z_n, rows, features), BF16),
            pltpu.VMEM((y_n, z_n, rows, hidden), BF16),
            pltpu.VMEM((y_n, z_n, rows, hidden), BF16),
            pltpu.VMEM((y_n, z_n, rows, features), BF16),
            pltpu.VMEM((features, hidden), F32),
            pltpu.VMEM((features, hidden), F32),
            dma((8,)),
            dma((2,)),
            dma((2, 2)),
            dma((2, 2)),
            dma((2,)),
            dma((2,)),
            dma((n_rings, 2, rounds)),
            dma((n_rings, 2, rounds)),
            dma((2, y_hi)),
            dma((2, y_hi)),
        ],
        compiler_params=pltpu.CompilerParams(
            collective_id=0, has_side_effects=True, vmem_limit_bytes=56 * 1024 * 1024
        ),
    )(
        sample_ids,
        embeddings,
        cotangent,
        w_up[0],
        w_down[0].T,
        b_up,
        b_down,
        ln_gain,
        ln_bias,
        fwd_store[0],
        bwd_store[0],
        fwd_scales[0].T,
        bwd_scales[0].T,
    )
    kept = pl.pallas_call(
        keep_kernel,
        out_shape=outs,
        in_specs=vmem(4),
        out_specs=tuple(vmem(4)),
    )(*results)
    return tuple(array[None] for array in kept)


def solution(mesh, y_hi=Y_HI):
    return jax.shard_map(
        functools.partial(per_device, mesh.shape["section"], mesh.shape["dp"], y_hi),
        mesh=mesh,
        in_specs=(
            P("dp", None),
            P("dp", None),
            P("section", "dp", "tensor"),
            P("section", "tensor", "dp"),
            P("section", "tensor"),
            P("section", None),
            P("section", None),
            P("section", None),
            P("section", "dp", None, None),
            P("section", "dp", None, None),
            P("dp"),
            P("section", "dp", None),
            P("section", "dp", None),
        ),
        out_specs=(
            P("section", "dp", None),
            P("section", "dp", None),
            P("section", "dp", "tensor"),
            P("section", "dp", "tensor"),
        ),
        check_vma=False,
    )
```

```python
import functools

import jax
import jax.numpy as jnp
from jax import lax
from jax.experimental import pallas as pl
from jax.experimental.pallas import tpu as pltpu
from jax.sharding import PartitionSpec as P

MESH = pl.DeviceIdType.MESH
BF16 = jnp.bfloat16
F32 = jnp.float32
Y_LO = 2
Y_HI = 4

root_half = 0.7071067811865476
density = 0.3989422804014327
epsilon = 1e-05


class Place:
    def __init__(self, n_dp, y_hi=Y_HI):
        self.y_hi_n = y_hi
        self.z_n = n_dp // y_hi
        self.y_n = y_hi * Y_LO
        self.dp = lax.axis_index("dp")
        self.lo = lax.axis_index("tensor")
        self.hi = self.dp // self.z_n
        self.z = self.dp % self.z_n
        self.y = self.hi * Y_LO + self.lo

    def at_y(self, y):
        return {"dp": (y // Y_LO) * self.z_n + self.z, "tensor": y % Y_LO}

    def at_z(self, z):
        return {"dp": self.hi * self.z_n + z, "tensor": self.lo}

    def step_y(self, d):
        return (self.y + d + self.y_n) % self.y_n

    def step_z(self, d):
        return (self.z + d + self.z_n) % self.z_n


def signal(barrier, device_id):
    pl.semaphore_signal(barrier, inc=1, device_id=device_id, device_id_type=MESH)


def remote(src, dst, send_sem, recv_sem, device_id):
    return pltpu.make_async_remote_copy(
        src_ref=src, dst_ref=dst, send_sem=send_sem, recv_sem=recv_sem, device_id=device_id, device_id_type=MESH
    )


class Ring:
    def __init__(self, n, step, slot, device, sems, index, last_way):
        self.step, self.slot, self.device = step, slot, device
        self.send_sem, self.recv_sem, self.index = sems[0], sems[1], index
        self.rounds = n // 2
        self.last_way = last_way

    def ways(self, r):
        return (self.last_way,) if r == self.rounds - 1 else (0, 1)

    def copy(self, way, r, received=False):
        sign = 1 - 2 * way
        block = self.slot(self.step(-sign * (r + 1 if received else r)))
        spot = (self.index, way, r)
        return remote(block, block, self.send_sem.at[spot], self.recv_sem.at[spot], self.device(self.step(sign)))

    def start(self, r):
        for way in self.ways(r):
            self.copy(way, r).start()

    def wait_recv(self, r):
        for way in self.ways(r):
            self.copy(way, r, True).wait_recv()

    def wait_send(self):
        for r in range(self.rounds):
            for way in self.ways(r):
                self.copy(way, r).wait_send()


class Spread:
    def __init__(self, n, step, part, slot, device, sems, index):
        self.step, self.part, self.slot, self.device = step, part, slot, device
        self.send_sem, self.recv_sem, self.index = sems[0], sems[1], index
        self.rounds = n // 2

    def ways(self, r):
        return (0,) if r == self.rounds - 1 else (0, 1)

    def copy(self, way, r, received=False):
        sign = 1 - 2 * way
        spot = (self.index, way, r)
        target = self.step(sign * (r + 1))
        block = self.slot(self.step(-sign * (r + 1) if received else 0))
        source = block if received else self.part(target)
        return remote(source, block, self.send_sem.at[spot], self.recv_sem.at[spot], self.device(target))

    wait_send = Ring.wait_send


def start_spreads(pairs):
    for r in range(max(pair[1].rounds for pair in pairs)):
        for pair in pairs:
            if r < pair[1].rounds:
                for way in pair[1].ways(r):
                    pair[1].copy(way, r).start()


def run_gathers(pairs, lag=1.0):
    free, events, count, missing, brought = {}, [], [0], {}, {}

    def push(ready, axis, ring, way, r, pair, size=1.0):
        begin = max(ready, free.get((axis, way), 0.0))
        free[axis, way] = begin + size
        count[0] += 1
        events.append((begin + size + lag, count[0], ring, way, r, pair))

    def go(ready, axis, ring, way, r, pair):
        push(ready, axis, ring, way, r, pair)
        ring.copy(way, r).start()

    def begin_chunk(ready, pair, d):
        for way in pair[3][d].ways(0):
            go(ready, pair[2], pair[3][d], way, 0, pair)

    def arrived(pair, n, d):
        key = (id(pair), d if d * 2 > -n else d + n)
        missing[key] = missing.get(key, len(pair[3])) - 1
        if missing[key] == 0 and pair[4] is not None:
            pair[4](d)

    for pair in pairs:
        spread = isinstance(pair[1], Spread)
        for r in range(pair[1].rounds if spread else 1):
            for way in pair[1].ways(r):
                if spread:
                    push(0.0, pair[0], pair[1], way, r, pair, r + 1.0)
                else:
                    go(0.0, pair[0], pair[1], way, r, pair)
    for pair in pairs:
        begin_chunk(0.0, pair, 0)
        arrived(pair, 2 * pair[3][0].rounds, 0)
    while events:
        event = min(events, key=lambda e: e[:2])
        events.remove(event)
        now, _, ring, way, r, pair = event
        ring.copy(way, r, True).wait_recv()
        d = -(r + 1) if way == 0 else r + 1
        first = ring is pair[1]
        if not (first and isinstance(ring, Spread)) and r + 1 < ring.rounds and way in ring.ways(r + 1):
            go(now, pair[0] if first else pair[2], ring, way, r + 1, pair)
        if first:
            begin_chunk(now, pair, d)
            arrived(pair, 2 * pair[3][0].rounds, 0)
        else:
            arrived(pair, 2 * ring.rounds, d)


def gelu_value(pre_gelu):
    return pre_gelu * 0.5 * (1.0 + lax.erf(pre_gelu * root_half))


def gelu_slope(pre_gelu):
    return (
        0.5 * (1.0 + lax.erf(pre_gelu * root_half))
        + pre_gelu * jnp.exp(-0.5 * pre_gelu * pre_gelu) * density
    )


def outer_t(left, right):
    return lax.dot_general(left, right, (((1,), (1,)), ((), ())), preferred_element_type=F32)


def inner(left, right):
    return lax.dot_general(left, right, (((0,), (0,)), ((), ())), preferred_element_type=F32)


def coded(values, base, bound):
    base = base.astype(F32)
    return (base + jnp.clip(values.astype(F32) - base, -bound, bound)).astype(BF16)


def layer_kernel(
    n_sections,
    n_dp,
    y_hi,
    sid_ref,
    emb_ref,
    cot_ref,
    up_ref,
    down_ref,
    bup_ref,
    bdown_ref,
    gain_ref,
    bias_ref,
    fst_ref,
    bst_ref,
    fsc_ref,
    bsc_ref,
    out_ref,
    ig_ref,
    up_out,
    down_out,
    up_all,
    down_all,
    bias_all,
    x_in,
    g_in,
    fst,
    bst,
    normed,
    act,
    pre_grad,
    out_rows,
    ig_rows,
    code_f,
    code_b,
    bound_f,
    bound_b,
    slope,
    unit,
    inv,
    scaled,
    normed_all,
    act_all,
    pg_all,
    g_all,
    up_block,
    down_block,
    load_sem,
    bias_sem,
    hop_send,
    hop_recv,
    peer_send,
    peer_recv,
    ring_send,
    ring_recv,
    out_send,
    out_recv,
):
    at = Place(n_dp, y_hi)
    section = lax.axis_index("section")
    rows, width = x_in.shape
    half = up_all.shape[2]
    features = normed_all.shape[3]
    hidden = act_all.shape[3]
    shard = up_ref.shape[0]
    wide = width // 2
    sems = (ring_send, ring_recv)
    mine = pl.ds(pl.multiple_of(at.lo * rows, rows), rows)
    other = pl.ds(pl.multiple_of((1 - at.lo) * rows, rows), rows)
    not_first = section > 0
    not_last = section < n_sections - 1
    early_first = section <= n_sections // 2
    early_after = jnp.logical_not(early_first)
    after = {"section": jnp.minimum(section + 1, n_sections - 1)}
    before = {"section": jnp.maximum(section - 1, 0)}
    peer = {"tensor": 1 - at.lo}
    owner_z = at.dp // at.y_hi_n

    barrier = pltpu.get_barrier_semaphore()
    for d in range(1, at.y_n):
        signal(barrier, at.at_y(at.step_y(d)))
    for d in range(1, at.z_n):
        signal(barrier, at.at_z(at.step_z(d)))
    for i in range(at.y_hi_n):
        source = i * at.z_n + owner_z

        @pl.when(source != at.dp)
        def _():
            signal(barrier, {"dp": source})

    @pl.when(not_first)
    def _():
        signal(barrier, before)

    @pl.when(not_last)
    def _():
        signal(barrier, after)

    own_rows = pl.ds(pl.multiple_of(at.dp * shard, shard), shard)
    own_up = pltpu.make_async_copy(up_ref, up_all.at[at.lo, own_rows], load_sem.at[0])
    own_down = pltpu.make_async_copy(down_ref, down_all.at[at.lo, own_rows], load_sem.at[1])
    load_fst = pltpu.make_async_copy(fst_ref.at[:, mine], fst, load_sem.at[2])
    load_bst = pltpu.make_async_copy(bst_ref.at[:, mine], bst, load_sem.at[3])
    load_emb = pltpu.make_async_copy(emb_ref.at[mine], x_in, load_sem.at[4])
    load_cot = pltpu.make_async_copy(cot_ref.at[mine], g_in, load_sem.at[5])
    own_up.start()
    own_down.start()
    load_fst.start()
    load_bst.start()

    @pl.when(section == 0)
    def _():
        load_emb.start()

    @pl.when(jnp.logical_not(not_last))
    def _():
        load_cot.start()

    bias_all[at.lo] = jnp.broadcast_to(bup_ref[...], bias_all.shape[1:])
    sends_self = jnp.int32(0)
    for i in range(at.y_hi_n):
        sends_self = sends_self + (at.z * at.y_hi_n + i == at.dp).astype(jnp.int32)
    sections_near = not_first.astype(jnp.int32) + not_last.astype(jnp.int32)
    own_up.wait()
    own_down.wait()
    pl.semaphore_wait(barrier, at.y_n + at.z_n - 2 + at.y_hi_n - sends_self + sections_near)

    bias_copy = remote(bias_all.at[at.lo], bias_all.at[at.lo], bias_sem.at[0], bias_sem.at[1], peer)
    bias_copy.start()

    def shard_rows(y, z):
        return pl.ds(pl.multiple_of(((y // Y_LO) * at.z_n + z) * shard, shard), shard)

    def up_slot(y, z):
        return up_all.at[y % Y_LO, shard_rows(y, z)]

    def down_slot(y, z):
        return down_all.at[y % Y_LO, shard_rows(y, z)]

    def fixed(slot, axis, step, d):
        there = step(d)
        return (lambda z: slot(there, z)) if axis == "y" else (lambda y: slot(y, there))

    y_ring = (at.y_n, at.step_y)
    z_ring = (at.z_n, at.step_z)
    up_first = Ring(*y_ring, fixed(up_slot, "z", at.step_z, 0), at.at_y, sems, 0, 0)
    down_first = Ring(*z_ring, fixed(down_slot, "y", at.step_y, 0), at.at_z, sems, 1, 1)
    up_then, down_then = {}, {}
    index = 2
    for d in range(-(at.y_n // 2), at.y_n // 2):
        up_then[d] = Ring(*z_ring, fixed(up_slot, "y", at.step_y, d), at.at_z, sems, index, index % 2)
        index += 1
    for d in range(-(at.z_n // 2), at.z_n // 2):
        down_then[d] = Ring(*y_ring, fixed(down_slot, "z", at.step_z, d), at.at_y, sems, index, index % 2)
        index += 1
    if down_first.last_way == 1:
        down_then[at.z_n // 2] = down_then.pop(-(at.z_n // 2))
    weight_rings = [up_first, down_first, *up_then.values(), *down_then.values()]
    run_gathers((("y", up_first, "z", up_then, None), ("z", down_first, "y", down_then, None)))

    scale_f = jnp.transpose(fsc_ref[...].astype(F32))
    scale_b = jnp.transpose(bsc_ref[...].astype(F32))
    low = at.lo == 0
    scale_f = 0.25 * jnp.where(low, scale_f[:rows], scale_f[rows:])
    scale_b = 0.25 * jnp.where(low, scale_b[:rows], scale_b[rows:])
    for b in range(fsc_ref.shape[0]):
        block = width // fsc_ref.shape[0]
        cols = pl.ds(b * block, block)
        bound_f[:, cols] = jnp.broadcast_to(scale_f[:, b : b + 1], (rows, block))
        bound_b[:, cols] = jnp.broadcast_to(scale_b[:, b : b + 1], (rows, block))
    remote(bias_all.at[1 - at.lo], bias_all.at[1 - at.lo], bias_sem.at[0], bias_sem.at[1], peer).wait_recv()
    bias_copy.wait_send()
    load_fst.wait()
    load_bst.wait()
    sid = sid_ref[0]

    def columns(j):
        return pl.ds(pl.multiple_of(j * wide, wide), wide)

    def fwd_copy(j):
        return remote(code_f.at[:, columns(j)], x_in.at[:, columns(j)], hop_send.at[0, j], hop_recv.at[0, j], after)

    def bwd_copy(j):
        return remote(code_b.at[:, columns(j)], g_in.at[:, columns(j)], hop_send.at[1, j], hop_recv.at[1, j], before)

    def hidden_half(h):
        return pl.ds(pl.multiple_of(h * half, half), half)

    def feature_cols(z):
        return pl.ds(pl.multiple_of(z * features, features), features)

    def hidden_cols(y):
        spot = (y % Y_LO) * at.y_hi_n + y // Y_LO
        return pl.ds(pl.multiple_of(spot * hidden, hidden), hidden)

    def exchange(src, dst, along_z, index, done=None):
        if along_z:
            spread = Spread(*z_ring, lambda z: src.at[:, feature_cols(z)], lambda z: dst.at[at.y, z], at.at_z, sems, index)
            there, ring, device = at.step_z, y_ring, at.at_y
        else:
            spread = Spread(*y_ring, lambda y: src.at[:, hidden_cols(y)], lambda y: dst.at[y, at.z], at.at_y, sems, index)
            there, ring, device = at.step_y, z_ring, at.at_z
        n = z_ring[0] if along_z else y_ring[0]
        rings = {}
        for d in range(1 - n // 2, n // 2 + 1):
            index += 1

            def slot(i, d=d):
                return dst.at[i, there(d)] if along_z else dst.at[there(d), i]

            rings[d if d < n // 2 else -d] = Ring(*ring, slot, device, sems, index, index % 2)
        axes = ("z", "y") if along_z else ("y", "z")
        return (axes[0], spread, axes[1], rings, done)

    def keep_own(src, dst, along_z):
        dst[at.y, at.z] = src[:, feature_cols(at.z)] if along_z else src[:, hidden_cols(at.y)]

    def add_column(d):
        z = at.step_z(d)
        left = normed_all[:, z].reshape(at.y_n * rows, features)
        up_block[...] += inner(left, pg_all[:, z].reshape(at.y_n * rows, hidden))

    def add_row(d):
        y = at.step_y(d)
        left = g_all[y].reshape(at.z_n * rows, features)
        down_block[...] += inner(left, act_all[y].reshape(at.z_n * rows, hidden))

    act_pair = exchange(act, act_all, False, index)
    normed_pair = exchange(normed, normed_all, True, index + 1 + at.y_n)
    pg_pair = exchange(pre_grad, pg_all, False, index + 2 + at.y_n + at.z_n, add_column)
    g_pair = exchange(g_in, g_all, True, index + 3 + 2 * at.y_n + at.z_n, add_row)
    early_pairs, late_pairs = (act_pair, normed_pair), (pg_pair, g_pair)

    def wait_sends(pairs):
        for pair in pairs:
            for ring in (pair[1], *pair[3].values()):
                ring.wait_send()

    def early_spreads():
        start_spreads(early_pairs)
        keep_own(act, act_all, False)
        keep_own(normed, normed_all, True)

    def early_sends():
        for ring in weight_rings:
            ring.wait_send()
        wait_sends(early_pairs)

    @pl.when(not_first)
    def _():
        for j in range(2):
            fwd_copy(j).wait_recv()

    @pl.when(section == 0)
    def _():
        load_emb.wait()

    values = x_in[...].astype(F32)
    centered = values - jnp.mean(values, axis=-1, keepdims=True)
    inverse = lax.rsqrt(jnp.mean(centered * centered, axis=-1, keepdims=True) + epsilon)
    unit_values = centered * inverse
    normed[...] = (unit_values * gain_ref[...] + bias_ref[...]).astype(BF16)
    unit[...] = unit_values
    inv[...] = jnp.broadcast_to(inverse, inv.shape)

    def up_half(h, _):
        pre = jnp.dot(normed[...], up_all[h], preferred_element_type=F32) + bias_all[h, 0:1, :]
        slope[:, hidden_half(h)] = pre
        act[:, hidden_half(h)] = gelu_value(pre).astype(BF16)
        return 0

    lax.fori_loop(0, 2, up_half, 0)

    def down_half(j, _):
        cols = columns(j)
        total = outer_t(act[:, :half], down_all[0, cols, :]) + outer_t(act[:, half:], down_all[1, cols, :])
        output = (x_in[:, cols].astype(F32) + total + bdown_ref[:, cols]).astype(BF16)
        out_rows[:, cols] = output
        code_f[:, cols] = coded(output, fst[sid, :, cols], bound_f[:, cols])

        @pl.when(not_last)
        def _():
            fwd_copy(j).start()

        return 0

    lax.fori_loop(0, 2, down_half, 0)
    out_keep = pltpu.make_async_copy(out_rows, out_ref.at[mine], load_sem.at[6])
    out_keep.start()
    out_copy = remote(out_rows, out_ref.at[mine], peer_send.at[0], peer_recv.at[0], peer)
    out_copy.start()

    def slope_half(h, _):
        slope[:, hidden_half(h)] = gelu_slope(slope[:, hidden_half(h)])
        return 0

    lax.fori_loop(0, 2, slope_half, 0)

    @pl.when(jnp.logical_or(early_first, not_last))
    def _():
        early_spreads()

    @pl.when(early_first)
    def _():
        run_gathers(early_pairs)
        early_sends()

    @pl.when(not_last)
    def _():
        for j in range(2):
            bwd_copy(j).wait_recv()

    @pl.when(jnp.logical_not(not_last))
    def _():
        load_cot.wait()

    def up_grad_half(h, _):
        act_grad = jnp.dot(g_in[...], down_all[h], preferred_element_type=F32)
        pre_grad[:, hidden_half(h)] = (act_grad * slope[:, hidden_half(h)]).astype(BF16)
        return 0

    lax.fori_loop(0, 2, up_grad_half, 0)
    start_spreads(late_pairs)
    keep_own(pre_grad, pg_all, False)
    keep_own(g_in, g_all, True)

    def norm_grad_half(j, _):
        cols = columns(j)
        total = outer_t(pre_grad[:, :half], up_all[0, cols, :]) + outer_t(pre_grad[:, half:], up_all[1, cols, :])
        scaled[:, cols] = total * gain_ref[:, cols]
        return 0

    lax.fori_loop(0, 2, norm_grad_half, 0)
    scaled_values = scaled[...]
    unit_values = unit[...]
    first_mean = jnp.mean(scaled_values, axis=-1, keepdims=True)
    second_mean = jnp.mean(scaled_values * unit_values, axis=-1, keepdims=True)

    for j in range(2):
        cols = pl.ds(j * wide, wide)
        inner_part = scaled[:, cols] - first_mean - unit[:, cols] * second_mean
        input_grad = (g_in[:, cols].astype(F32) + inv[:, 0:1] * inner_part).astype(BF16)
        ig_rows[:, cols] = input_grad
        code_b[:, cols] = coded(input_grad, bst[sid, :, cols], bound_b[:, cols])

        @pl.when(not_first)
        def _():
            bwd_copy(j).start()

    ig_keep = pltpu.make_async_copy(ig_rows, ig_ref.at[mine], load_sem.at[7])
    ig_keep.start()
    ig_copy = remote(ig_rows, ig_ref.at[mine], peer_send.at[1], peer_recv.at[1], peer)
    ig_copy.start()

    @pl.when(jnp.logical_and(early_after, jnp.logical_not(not_last)))
    def _():
        early_spreads()

    up_block[...] = jnp.zeros_like(up_block)
    down_block[...] = jnp.zeros_like(down_block)
    @pl.when(early_first)
    def _():
        run_gathers(late_pairs)

    @pl.when(early_after)
    def _():
        run_gathers([pair[:4] + (None,) for pair in late_pairs + early_pairs])
        lax.fori_loop(0, at.z_n, lambda d, _: (add_column(d), 0)[1], 0)
        lax.fori_loop(0, at.y_n, lambda d, _: (add_row(d), 0)[1], 0)
        early_sends()

    out_cols = pl.ds(pl.multiple_of(at.hi * hidden, hidden), hidden)
    outs = ((0, up_block, up_out), (1, down_block, down_out))

    def grad_copy(k, block, out, i):
        return remote(
            block.at[pl.ds(i * shard, shard)],
            out.at[:, out_cols],
            out_send.at[k, i],
            out_recv.at[k, at.hi],
            {"dp": at.z * at.y_hi_n + i},
        )

    def grad_keep(k, block, out, i):
        return pltpu.make_async_copy(block.at[pl.ds(i * shard, shard)], out.at[:, out_cols], out_send.at[k, i])

    for i in range(at.y_hi_n):
        own = at.z * at.y_hi_n + i == at.dp

        @pl.when(jnp.logical_not(own))
        def _():
            for k, block, out in outs:
                grad_copy(k, block, out, i).start()

        @pl.when(own)
        def _():
            for k, block, out in outs:
                grad_keep(k, block, out, i).start()

    @pl.when(not_last)
    def _():
        for j in range(2):
            fwd_copy(j).wait_send()

    @pl.when(not_first)
    def _():
        for j in range(2):
            bwd_copy(j).wait_send()

    wait_sends(late_pairs)
    remote(out_rows, out_ref.at[other], peer_send.at[0], peer_recv.at[0], peer).wait_recv()
    remote(ig_rows, ig_ref.at[other], peer_send.at[1], peer_recv.at[1], peer).wait_recv()
    out_copy.wait_send()
    ig_copy.wait_send()
    out_keep.wait()
    ig_keep.wait()

    for i in range(at.y_hi_n):

        @pl.when(i * at.z_n + owner_z != at.dp)
        def _():
            for k, block, out in outs:
                spot = out.at[:, pl.ds(i * hidden, hidden)]
                remote(spot, spot, out_send.at[k, 0], out_recv.at[k, i], {"dp": at.z * at.y_hi_n + i}).wait_recv()

    for i in range(at.y_hi_n):
        own = at.z * at.y_hi_n + i == at.dp

        @pl.when(jnp.logical_not(own))
        def _():
            for k, block, out in outs:
                grad_copy(k, block, out, i).wait_send()

        @pl.when(own)
        def _():
            for k, block, out in outs:
                grad_keep(k, block, out, i).wait()


def keep_kernel(*refs):
    count = len(refs) // 2
    for source, target in zip(refs[:count], refs[count:]):
        target[...] = source[...]


def vmem(count):
    return [pl.BlockSpec(memory_space=pltpu.VMEM)] * count


def anywhere(count):
    return [pl.BlockSpec(memory_space=pl.ANY)] * count


def per_device(
    n_sections,
    n_dp,
    y_hi,
    embeddings,
    cotangent,
    w_up,
    w_down,
    b_up,
    b_down,
    ln_gain,
    ln_bias,
    fwd_store,
    bwd_store,
    sample_ids,
    fwd_scales,
    bwd_scales,
):
    z_n = n_dp // y_hi
    y_n = y_hi * Y_LO
    shard, half = w_up.shape[1:]
    width = embeddings.shape[1]
    rows = embeddings.shape[0] // Y_LO
    hidden_all = Y_LO * half
    features = width // z_n
    hidden = hidden_all // y_n
    stored = fwd_store.shape[1]
    dma = pltpu.SemaphoreType.DMA
    rounds = max(y_n, z_n) // 2
    n_rings = 6 + 3 * (y_n + z_n)
    whole = pltpu.VMEM((Y_LO, width, half), BF16)
    narrow = pltpu.VMEM((rows, width), BF16)
    wide = pltpu.VMEM((rows, width), F32)
    outs = (
        jax.ShapeDtypeStruct(embeddings.shape, BF16),
        jax.ShapeDtypeStruct(embeddings.shape, BF16),
        jax.ShapeDtypeStruct((shard, half), F32),
        jax.ShapeDtypeStruct((shard, half), F32),
    )
    results = pl.pallas_call(
        functools.partial(layer_kernel, n_sections, n_dp, y_hi),
        out_shape=outs,
        in_specs=[pl.BlockSpec(memory_space=pltpu.SMEM)] + anywhere(4) + vmem(4) + anywhere(2) + vmem(2),
        out_specs=tuple(anywhere(4)),
        scratch_shapes=[
            whole,
            whole,
            pltpu.VMEM((Y_LO, 8, half), F32),
            narrow,
            narrow,
            pltpu.VMEM((stored, rows, width), BF16),
            pltpu.VMEM((stored, rows, width), BF16),
            narrow,
            pltpu.VMEM((rows, hidden_all), BF16),
            pltpu.VMEM((rows, hidden_all), BF16),
            narrow,
            narrow,
            narrow,
            narrow,
            wide,
            wide,
            pltpu.VMEM((rows, hidden_all), F32),
            wide,
            pltpu.VMEM((rows, 128), F32),
            wide,
            pltpu.VMEM((y_n, z_n, rows, features), BF16),
            pltpu.VMEM((y_n, z_n, rows, hidden), BF16),
            pltpu.VMEM((y_n, z_n, rows, hidden), BF16),
            pltpu.VMEM((y_n, z_n, rows, features), BF16),
            pltpu.VMEM((features, hidden), F32),
            pltpu.VMEM((features, hidden), F32),
            dma((8,)),
            dma((2,)),
            dma((2, 2)),
            dma((2, 2)),
            dma((2,)),
            dma((2,)),
            dma((n_rings, 2, rounds)),
            dma((n_rings, 2, rounds)),
            dma((2, y_hi)),
            dma((2, y_hi)),
        ],
        compiler_params=pltpu.CompilerParams(
            collective_id=0, has_side_effects=True, vmem_limit_bytes=56 * 1024 * 1024
        ),
    )(
        sample_ids,
        embeddings,
        cotangent,
        w_up[0],
        w_down[0].T,
        b_up,
        b_down,
        ln_gain,
        ln_bias,
        fwd_store[0],
        bwd_store[0],
        fwd_scales[0].T,
        bwd_scales[0].T,
    )
    kept = pl.pallas_call(
        keep_kernel,
        out_shape=outs,
        in_specs=vmem(4),
        out_specs=tuple(vmem(4)),
    )(*results)
    return tuple(array[None] for array in kept)


def solution(mesh, y_hi=Y_HI):
    return jax.shard_map(
        functools.partial(per_device, mesh.shape["section"], mesh.shape["dp"], y_hi),
        mesh=mesh,
        in_specs=(
            P("dp", None),
            P("dp", None),
            P("section", "dp", "tensor"),
            P("section", "tensor", "dp"),
            P("section", "tensor"),
            P("section", None),
            P("section", None),
            P("section", None),
            P("section", "dp", None, None),
            P("section", "dp", None, None),
            P("dp"),
            P("section", "dp", None),
            P("section", "dp", None),
        ),
        out_specs=(
            P("section", "dp", None),
            P("section", "dp", None),
            P("section", "dp", "tensor"),
            P("section", "dp", "tensor"),
        ),
        check_vma=False,
    )
```

```python
import functools

import jax
import jax.numpy as jnp
from jax import lax
from jax.experimental import pallas as pl
from jax.experimental.pallas import tpu as pltpu
from jax.sharding import PartitionSpec as P

MESH = pl.DeviceIdType.MESH
BF16 = jnp.bfloat16
F32 = jnp.float32
Y_LO = 2
Y_HI = 4
TURN = 24

root_half = 0.7071067811865476
density = 0.3989422804014327
epsilon = 1e-05


class Place:
    def __init__(self, n_dp, y_hi=Y_HI):
        self.y_hi_n = y_hi
        self.z_n = n_dp // y_hi
        self.y_n = y_hi * Y_LO
        self.dp = lax.axis_index("dp")
        self.lo = lax.axis_index("tensor")
        self.hi = self.dp // self.z_n
        self.z = self.dp % self.z_n
        self.y = self.hi * Y_LO + self.lo

    def at_y(self, y):
        return {"dp": (y // Y_LO) * self.z_n + self.z, "tensor": y % Y_LO}

    def at_z(self, z):
        return {"dp": self.hi * self.z_n + z, "tensor": self.lo}

    def step_y(self, d):
        return (self.y + d + self.y_n) % self.y_n

    def step_z(self, d):
        return (self.z + d + self.z_n) % self.z_n


def signal(barrier, device_id):
    pl.semaphore_signal(barrier, inc=1, device_id=device_id, device_id_type=MESH)


def remote(src, dst, send_sem, recv_sem, device_id):
    return pltpu.make_async_remote_copy(
        src_ref=src, dst_ref=dst, send_sem=send_sem, recv_sem=recv_sem, device_id=device_id, device_id_type=MESH
    )


class Ring:
    def __init__(self, n, step, slot, device, sems, index, last_way):
        self.step, self.slot, self.device = step, slot, device
        self.send_sem, self.recv_sem, self.index = sems[0], sems[1], index
        self.rounds = n // 2
        self.last_way = last_way

    def ways(self, r):
        return (self.last_way,) if r == self.rounds - 1 else (0, 1)

    def copy(self, way, r, received=False):
        sign = 1 - 2 * way
        block = self.slot(self.step(-sign * (r + 1 if received else r)))
        spot = (self.index, way, r)
        return remote(block, block, self.send_sem.at[spot], self.recv_sem.at[spot], self.device(self.step(sign)))

    def start(self, r):
        for way in self.ways(r):
            self.copy(way, r).start()

    def wait_recv(self, r):
        for way in self.ways(r):
            self.copy(way, r, True).wait_recv()

    def wait_send(self):
        for r in range(self.rounds):
            for way in self.ways(r):
                self.copy(way, r).wait_send()


class Spread:
    def __init__(self, n, step, part, slot, device, sems, index):
        self.step, self.part, self.slot, self.device = step, part, slot, device
        self.send_sem, self.recv_sem, self.index = sems[0], sems[1], index
        self.rounds = n // 2

    def ways(self, r):
        return (0,) if r == self.rounds - 1 else (0, 1)

    def copy(self, way, r, received=False):
        sign = 1 - 2 * way
        spot = (self.index, way, r)
        target = self.step(sign * (r + 1))
        block = self.slot(self.step(-sign * (r + 1) if received else 0))
        source = block if received else self.part(target)
        return remote(source, block, self.send_sem.at[spot], self.recv_sem.at[spot], self.device(target))

    wait_send = Ring.wait_send


def start_spreads(pairs):
    for r in range(max(pair[1].rounds for pair in pairs)):
        for pair in pairs:
            if r < pair[1].rounds:
                for way in pair[1].ways(r):
                    pair[1].copy(way, r).start()


def run_gathers(pairs, lag=1.0, midway=None):
    free, events, count, missing, brought = {}, [], [0], {}, {}

    def push(ready, axis, ring, way, r, pair, size=1.0):
        begin = max(ready, free.get((axis, way), 0.0))
        free[axis, way] = begin + size
        count[0] += 1
        events.append((begin + size + lag, count[0], ring, way, r, pair))

    def go(ready, axis, ring, way, r, pair):
        push(ready, axis, ring, way, r, pair)
        ring.copy(way, r).start()

    def begin_chunk(ready, pair, d):
        for way in pair[3][d].ways(0):
            go(ready, pair[2], pair[3][d], way, 0, pair)

    def arrived(pair, n, d):
        key = (id(pair), d if d * 2 > -n else d + n)
        missing[key] = missing.get(key, len(pair[3])) - 1
        if missing[key] == 0 and pair[4] is not None:
            pair[4](d)

    for pair in pairs:
        spread = isinstance(pair[1], Spread)
        for r in range(pair[1].rounds if spread else 1):
            for way in pair[1].ways(r):
                if spread:
                    push(0.0, pair[0], pair[1], way, r, pair, r + 1.0)
                else:
                    go(0.0, pair[0], pair[1], way, r, pair)
    for pair in pairs:
        begin_chunk(0.0, pair, 0)
        arrived(pair, 2 * pair[3][0].rounds, 0)
    arrivals = 0
    while events:
        event = min(events, key=lambda e: e[:2])
        events.remove(event)
        now, _, ring, way, r, pair = event
        ring.copy(way, r, True).wait_recv()
        d = -(r + 1) if way == 0 else r + 1
        arrivals += 1
        if midway is not None and arrivals == midway[0]:
            midway[1]()
        first = ring is pair[1]
        if not (first and isinstance(ring, Spread)) and r + 1 < ring.rounds and way in ring.ways(r + 1):
            go(now, pair[0] if first else pair[2], ring, way, r + 1, pair)
        if first:
            begin_chunk(now, pair, d)
            arrived(pair, 2 * pair[3][0].rounds, 0)
        else:
            arrived(pair, 2 * ring.rounds, d)


def gelu_value(pre_gelu):
    return pre_gelu * 0.5 * (1.0 + lax.erf(pre_gelu * root_half))


def gelu_slope(pre_gelu):
    return (
        0.5 * (1.0 + lax.erf(pre_gelu * root_half))
        + pre_gelu * jnp.exp(-0.5 * pre_gelu * pre_gelu) * density
    )


def outer_t(left, right):
    return lax.dot_general(left, right, (((1,), (1,)), ((), ())), preferred_element_type=F32)


def inner(left, right):
    return lax.dot_general(left, right, (((0,), (0,)), ((), ())), preferred_element_type=F32)


def coded(values, base, bound):
    base = base.astype(F32)
    return (base + jnp.clip(values.astype(F32) - base, -bound, bound)).astype(BF16)


def layer_kernel(
    n_sections,
    n_dp,
    y_hi,
    sid_ref,
    emb_ref,
    cot_ref,
    up_ref,
    down_ref,
    bup_ref,
    bdown_ref,
    gain_ref,
    bias_ref,
    fst_ref,
    bst_ref,
    fsc_ref,
    bsc_ref,
    out_ref,
    ig_ref,
    up_out,
    down_out,
    up_all,
    down_all,
    up_turned,
    down_turned,
    bias_all,
    x_in,
    g_in,
    fst,
    bst,
    normed,
    act,
    pre_grad,
    out_rows,
    ig_rows,
    code_f,
    code_b,
    bound_f,
    bound_b,
    slope,
    unit,
    inv,
    scaled,
    normed_all,
    act_all,
    pg_all,
    g_all,
    up_block,
    down_block,
    load_sem,
    turn_sem,
    bias_sem,
    hop_send,
    hop_recv,
    peer_send,
    peer_recv,
    ring_send,
    ring_recv,
    out_send,
    out_recv,
):
    at = Place(n_dp, y_hi)
    section = lax.axis_index("section")
    rows, width = x_in.shape
    half = up_all.shape[2]
    features = normed_all.shape[3]
    hidden = act_all.shape[3]
    shard = up_ref.shape[0]
    wide = width // 2
    sems = (ring_send, ring_recv)
    mine = pl.ds(pl.multiple_of(at.lo * rows, rows), rows)
    other = pl.ds(pl.multiple_of((1 - at.lo) * rows, rows), rows)
    not_first = section > 0
    not_last = section < n_sections - 1
    early_first = section <= n_sections // 2
    early_after = jnp.logical_not(early_first)
    after = {"section": jnp.minimum(section + 1, n_sections - 1)}
    before = {"section": jnp.maximum(section - 1, 0)}
    peer = {"tensor": 1 - at.lo}
    owner_z = at.dp // at.y_hi_n

    barrier = pltpu.get_barrier_semaphore()
    for d in range(1, at.y_n):
        signal(barrier, at.at_y(at.step_y(d)))
    for d in range(1, at.z_n):
        signal(barrier, at.at_z(at.step_z(d)))
    for i in range(at.y_hi_n):
        source = i * at.z_n + owner_z

        @pl.when(source != at.dp)
        def _():
            signal(barrier, {"dp": source})

    @pl.when(not_first)
    def _():
        signal(barrier, before)

    @pl.when(not_last)
    def _():
        signal(barrier, after)

    own_rows = pl.ds(pl.multiple_of(at.dp * shard, shard), shard)
    own_up = pltpu.make_async_copy(up_ref, up_all.at[at.lo, own_rows], load_sem.at[0])
    own_down = pltpu.make_async_copy(down_ref, down_all.at[at.lo, own_rows], load_sem.at[1])
    load_fst = pltpu.make_async_copy(fst_ref.at[:, mine], fst, load_sem.at[2])
    load_bst = pltpu.make_async_copy(bst_ref.at[:, mine], bst, load_sem.at[3])
    load_emb = pltpu.make_async_copy(emb_ref.at[mine], x_in, load_sem.at[4])
    load_cot = pltpu.make_async_copy(cot_ref.at[mine], g_in, load_sem.at[5])
    own_up.start()
    own_down.start()
    load_fst.start()
    load_bst.start()

    @pl.when(section == 0)
    def _():
        load_emb.start()

    @pl.when(jnp.logical_not(not_last))
    def _():
        load_cot.start()

    bias_all[at.lo] = jnp.broadcast_to(bup_ref[...], bias_all.shape[1:])
    sends_self = jnp.int32(0)
    for i in range(at.y_hi_n):
        sends_self = sends_self + (at.z * at.y_hi_n + i == at.dp).astype(jnp.int32)
    sections_near = not_first.astype(jnp.int32) + not_last.astype(jnp.int32)
    own_up.wait()
    own_down.wait()
    pl.semaphore_wait(barrier, at.y_n + at.z_n - 2 + at.y_hi_n - sends_self + sections_near)

    bias_copy = remote(bias_all.at[at.lo], bias_all.at[at.lo], bias_sem.at[0], bias_sem.at[1], peer)
    bias_copy.start()

    def shard_rows(y, z):
        return pl.ds(pl.multiple_of(((y // Y_LO) * at.z_n + z) * shard, shard), shard)

    def up_slot(y, z):
        return up_all.at[y % Y_LO, shard_rows(y, z)]

    def down_slot(y, z):
        return down_all.at[y % Y_LO, shard_rows(y, z)]

    def fixed(slot, axis, step, d):
        there = step(d)
        return (lambda z: slot(there, z)) if axis == "y" else (lambda y: slot(y, there))

    y_ring = (at.y_n, at.step_y)
    z_ring = (at.z_n, at.step_z)
    up_first = Ring(*y_ring, fixed(up_slot, "z", at.step_z, 0), at.at_y, sems, 0, 0)
    down_first = Ring(*z_ring, fixed(down_slot, "y", at.step_y, 0), at.at_z, sems, 1, 1)
    up_then, down_then = {}, {}
    index = 2
    for d in range(-(at.y_n // 2), at.y_n // 2):
        up_then[d] = Ring(*z_ring, fixed(up_slot, "y", at.step_y, d), at.at_z, sems, index, index % 2)
        index += 1
    for d in range(-(at.z_n // 2), at.z_n // 2):
        down_then[d] = Ring(*y_ring, fixed(down_slot, "z", at.step_z, d), at.at_y, sems, index, index % 2)
        index += 1
    if down_first.last_way == 1:
        down_then[at.z_n // 2] = down_then.pop(-(at.z_n // 2))
    weight_rings = [up_first, down_first, *up_then.values(), *down_then.values()]
    weight_pairs = (("y", up_first, "z", up_then, None), ("z", down_first, "y", down_then, None))
    even = section % 2 == 0

    @pl.when(jnp.logical_not(even))
    def _():
        pl.semaphore_wait(turn_sem, 1)

    def pass_turn():
        @pl.when(jnp.logical_and(even, not_last))
        def _():
            pl.semaphore_signal(turn_sem, inc=1, device_id=after, device_id_type=MESH)

    run_gathers(weight_pairs, midway=(TURN, pass_turn))

    scale_f = jnp.transpose(fsc_ref[...].astype(F32))
    scale_b = jnp.transpose(bsc_ref[...].astype(F32))
    low = at.lo == 0
    scale_f = 0.25 * jnp.where(low, scale_f[:rows], scale_f[rows:])
    scale_b = 0.25 * jnp.where(low, scale_b[:rows], scale_b[rows:])
    for b in range(fsc_ref.shape[0]):
        block = width // fsc_ref.shape[0]
        cols = pl.ds(b * block, block)
        bound_f[:, cols] = jnp.broadcast_to(scale_f[:, b : b + 1], (rows, block))
        bound_b[:, cols] = jnp.broadcast_to(scale_b[:, b : b + 1], (rows, block))
    remote(bias_all.at[1 - at.lo], bias_all.at[1 - at.lo], bias_sem.at[0], bias_sem.at[1], peer).wait_recv()
    bias_copy.wait_send()
    load_fst.wait()
    load_bst.wait()
    sid = sid_ref[0]

    def columns(j):
        return pl.ds(pl.multiple_of(j * wide, wide), wide)

    def fwd_copy(j):
        return remote(code_f.at[:, columns(j)], x_in.at[:, columns(j)], hop_send.at[0, j], hop_recv.at[0, j], after)

    def bwd_copy(j):
        return remote(code_b.at[:, columns(j)], g_in.at[:, columns(j)], hop_send.at[1, j], hop_recv.at[1, j], before)

    def hidden_half(h):
        return pl.ds(pl.multiple_of(h * half, half), half)

    def feature_cols(z):
        return pl.ds(pl.multiple_of(z * features, features), features)

    def hidden_cols(y):
        spot = (y % Y_LO) * at.y_hi_n + y // Y_LO
        return pl.ds(pl.multiple_of(spot * hidden, hidden), hidden)

    def exchange(src, dst, along_z, index, done=None):
        if along_z:
            spread = Spread(*z_ring, lambda z: src.at[:, feature_cols(z)], lambda z: dst.at[at.y, z], at.at_z, sems, index)
            there, ring, device = at.step_z, y_ring, at.at_y
        else:
            spread = Spread(*y_ring, lambda y: src.at[:, hidden_cols(y)], lambda y: dst.at[y, at.z], at.at_y, sems, index)
            there, ring, device = at.step_y, z_ring, at.at_z
        n = z_ring[0] if along_z else y_ring[0]
        rings = {}
        for d in range(1 - n // 2, n // 2 + 1):
            index += 1

            def slot(i, d=d):
                return dst.at[i, there(d)] if along_z else dst.at[there(d), i]

            rings[d if d < n // 2 else -d] = Ring(*ring, slot, device, sems, index, index % 2)
        axes = ("z", "y") if along_z else ("y", "z")
        return (axes[0], spread, axes[1], rings, done)

    def keep_own(src, dst, along_z):
        dst[at.y, at.z] = src[:, feature_cols(at.z)] if along_z else src[:, hidden_cols(at.y)]

    def add_column(d):
        z = at.step_z(d)
        left = normed_all[:, z].reshape(at.y_n * rows, features)
        up_block[...] += inner(left, pg_all[:, z].reshape(at.y_n * rows, hidden))

    def add_row(d):
        y = at.step_y(d)
        left = g_all[y].reshape(at.z_n * rows, features)
        down_block[...] += inner(left, act_all[y].reshape(at.z_n * rows, hidden))

    act_pair = exchange(act, act_all, False, index)
    normed_pair = exchange(normed, normed_all, True, index + 1 + at.y_n)
    pg_pair = exchange(pre_grad, pg_all, False, index + 2 + at.y_n + at.z_n, add_column)
    g_pair = exchange(g_in, g_all, True, index + 3 + 2 * at.y_n + at.z_n, add_row)
    early_pairs, late_pairs = (act_pair, normed_pair), (pg_pair, g_pair)

    def wait_sends(pairs):
        for pair in pairs:
            for ring in (pair[1], *pair[3].values()):
                ring.wait_send()

    def early_spreads():
        start_spreads(early_pairs)
        keep_own(act, act_all, False)
        keep_own(normed, normed_all, True)

    def early_sends():
        for ring in weight_rings:
            ring.wait_send()
        wait_sends(early_pairs)

    def turn(source, target):
        count = half // 128

        def body(i, _):
            cols = pl.ds(pl.multiple_of((i % count) * 128, 128), 128)
            target[i // count, cols, :] = jnp.transpose(source[i // count, :, cols])
            return 0

        lax.fori_loop(0, 2 * count, body, 0)

    @pl.when(not_first)
    def _():
        turn(down_all, down_turned)

    @pl.when(section > 1)
    def _():
        turn(up_all, up_turned)

    @pl.when(not_first)
    def _():
        for j in range(2):
            fwd_copy(j).wait_recv()

    @pl.when(section == 0)
    def _():
        load_emb.wait()

    values = x_in[...].astype(F32)
    centered = values - jnp.mean(values, axis=-1, keepdims=True)
    inverse = lax.rsqrt(jnp.mean(centered * centered, axis=-1, keepdims=True) + epsilon)
    unit_values = centered * inverse
    normed[...] = (unit_values * gain_ref[...] + bias_ref[...]).astype(BF16)
    unit[...] = unit_values
    inv[...] = jnp.broadcast_to(inverse, inv.shape)

    for h in range(2):
        spot = pl.ds(h * half, half)
        pre = jnp.dot(normed[...], up_all[h], preferred_element_type=F32) + bias_all[h, 0:1, :]
        slope[:, spot] = pre
        act[:, spot] = gelu_value(pre).astype(BF16)

    def finish_output(j, total):
        cols = pl.ds(j * wide, wide)
        output = (x_in[:, cols].astype(F32) + total + bdown_ref[:, cols]).astype(BF16)
        out_rows[:, cols] = output
        code_f[:, cols] = coded(output, fst[sid, :, cols], bound_f[:, cols])

        @pl.when(not_last)
        def _():
            fwd_copy(j).start()

    def product_t(left, right, j):
        cols = pl.ds(j * wide, wide)
        return outer_t(left[:, :half], right[0, cols, :]) + outer_t(left[:, half:], right[1, cols, :])

    def product(left, right, j):
        cols = pl.ds(j * wide, wide)
        return jnp.dot(left[:, :half], right[0, :, cols], preferred_element_type=F32) + jnp.dot(
            left[:, half:], right[1, :, cols], preferred_element_type=F32
        )

    @pl.when(section == 0)
    def _():
        for j in range(2):
            finish_output(j, product_t(act, down_all, j))

    @pl.when(not_first)
    def _():
        for j in range(2):
            finish_output(j, product(act, down_turned, j))

    out_keep = pltpu.make_async_copy(out_rows, out_ref.at[mine], load_sem.at[6])
    out_keep.start()
    out_copy = remote(out_rows, out_ref.at[mine], peer_send.at[0], peer_recv.at[0], peer)
    out_copy.start()

    @pl.when(section <= 1)
    def _():
        turn(up_all, up_turned)

    def slope_half(h, _):
        slope[:, hidden_half(h)] = gelu_slope(slope[:, hidden_half(h)])
        return 0

    lax.fori_loop(0, 2, slope_half, 0)

    @pl.when(jnp.logical_or(early_first, not_last))
    def _():
        early_spreads()

    @pl.when(early_first)
    def _():
        run_gathers(early_pairs)
        early_sends()

    @pl.when(not_last)
    def _():
        for j in range(2):
            bwd_copy(j).wait_recv()

    @pl.when(jnp.logical_not(not_last))
    def _():
        load_cot.wait()

    for h in range(2):
        spot = pl.ds(h * half, half)
        act_grad = jnp.dot(g_in[...], down_all[h], preferred_element_type=F32)
        pre_grad[:, spot] = (act_grad * slope[:, spot]).astype(BF16)

    def late_spreads():
        start_spreads(late_pairs)
        keep_own(pre_grad, pg_all, False)
        keep_own(g_in, g_all, True)

    @pl.when(section == 0)
    def _():
        late_spreads()

    for j in range(2):
        cols = pl.ds(j * wide, wide)
        scaled[:, cols] = product(pre_grad, up_turned, j) * gain_ref[:, cols]
    scaled_values = scaled[...]
    unit_values = unit[...]
    first_mean = jnp.mean(scaled_values, axis=-1, keepdims=True)
    second_mean = jnp.mean(scaled_values * unit_values, axis=-1, keepdims=True)

    for j in range(2):
        cols = pl.ds(j * wide, wide)
        inner_part = scaled[:, cols] - first_mean - unit[:, cols] * second_mean
        input_grad = (g_in[:, cols].astype(F32) + inv[:, 0:1] * inner_part).astype(BF16)
        ig_rows[:, cols] = input_grad
        code_b[:, cols] = coded(input_grad, bst[sid, :, cols], bound_b[:, cols])

        @pl.when(not_first)
        def _():
            bwd_copy(j).start()

    @pl.when(not_first)
    def _():
        late_spreads()

    ig_keep = pltpu.make_async_copy(ig_rows, ig_ref.at[mine], load_sem.at[7])
    ig_keep.start()
    ig_copy = remote(ig_rows, ig_ref.at[mine], peer_send.at[1], peer_recv.at[1], peer)
    ig_copy.start()

    @pl.when(jnp.logical_and(early_after, jnp.logical_not(not_last)))
    def _():
        early_spreads()

    up_block[...] = jnp.zeros_like(up_block)
    down_block[...] = jnp.zeros_like(down_block)
    @pl.when(early_first)
    def _():
        run_gathers(late_pairs)

    @pl.when(early_after)
    def _():
        run_gathers([pair[:4] + (None,) for pair in late_pairs + early_pairs])
        lax.fori_loop(0, at.z_n, lambda d, _: (add_column(d), 0)[1], 0)
        lax.fori_loop(0, at.y_n, lambda d, _: (add_row(d), 0)[1], 0)
        early_sends()

    out_cols = pl.ds(pl.multiple_of(at.hi * hidden, hidden), hidden)
    outs = ((0, up_block, up_out), (1, down_block, down_out))

    def grad_copy(k, block, out, i):
        return remote(
            block.at[pl.ds(i * shard, shard)],
            out.at[:, out_cols],
            out_send.at[k, i],
            out_recv.at[k, at.hi],
            {"dp": at.z * at.y_hi_n + i},
        )

    def grad_keep(k, block, out, i):
        return pltpu.make_async_copy(block.at[pl.ds(i * shard, shard)], out.at[:, out_cols], out_send.at[k, i])

    for i in range(at.y_hi_n):
        own = at.z * at.y_hi_n + i == at.dp

        @pl.when(jnp.logical_not(own))
        def _():
            for k, block, out in outs:
                grad_copy(k, block, out, i).start()

        @pl.when(own)
        def _():
            for k, block, out in outs:
                grad_keep(k, block, out, i).start()

    @pl.when(not_last)
    def _():
        for j in range(2):
            fwd_copy(j).wait_send()

    @pl.when(not_first)
    def _():
        for j in range(2):
            bwd_copy(j).wait_send()

    wait_sends(late_pairs)
    remote(out_rows, out_ref.at[other], peer_send.at[0], peer_recv.at[0], peer).wait_recv()
    remote(ig_rows, ig_ref.at[other], peer_send.at[1], peer_recv.at[1], peer).wait_recv()
    out_copy.wait_send()
    ig_copy.wait_send()
    out_keep.wait()
    ig_keep.wait()

    for i in range(at.y_hi_n):

        @pl.when(i * at.z_n + owner_z != at.dp)
        def _():
            for k, block, out in outs:
                spot = out.at[:, pl.ds(i * hidden, hidden)]
                remote(spot, spot, out_send.at[k, 0], out_recv.at[k, i], {"dp": at.z * at.y_hi_n + i}).wait_recv()

    for i in range(at.y_hi_n):
        own = at.z * at.y_hi_n + i == at.dp

        @pl.when(jnp.logical_not(own))
        def _():
            for k, block, out in outs:
                grad_copy(k, block, out, i).wait_send()

        @pl.when(own)
        def _():
            for k, block, out in outs:
                grad_keep(k, block, out, i).wait()


def keep_kernel(*refs):
    count = len(refs) // 2
    for source, target in zip(refs[:count], refs[count:]):
        target[...] = source[...]


def vmem(count):
    return [pl.BlockSpec(memory_space=pltpu.VMEM)] * count


def anywhere(count):
    return [pl.BlockSpec(memory_space=pl.ANY)] * count


def per_device(
    n_sections,
    n_dp,
    y_hi,
    embeddings,
    cotangent,
    w_up,
    w_down,
    b_up,
    b_down,
    ln_gain,
    ln_bias,
    fwd_store,
    bwd_store,
    sample_ids,
    fwd_scales,
    bwd_scales,
):
    z_n = n_dp // y_hi
    y_n = y_hi * Y_LO
    shard, half = w_up.shape[1:]
    width = embeddings.shape[1]
    rows = embeddings.shape[0] // Y_LO
    hidden_all = Y_LO * half
    features = width // z_n
    hidden = hidden_all // y_n
    stored = fwd_store.shape[1]
    dma = pltpu.SemaphoreType.DMA
    rounds = max(y_n, z_n) // 2
    n_rings = 6 + 3 * (y_n + z_n)
    whole = pltpu.VMEM((Y_LO, width, half), BF16)
    narrow = pltpu.VMEM((rows, width), BF16)
    wide = pltpu.VMEM((rows, width), F32)
    outs = (
        jax.ShapeDtypeStruct(embeddings.shape, BF16),
        jax.ShapeDtypeStruct(embeddings.shape, BF16),
        jax.ShapeDtypeStruct((shard, half), F32),
        jax.ShapeDtypeStruct((shard, half), F32),
    )
    results = pl.pallas_call(
        functools.partial(layer_kernel, n_sections, n_dp, y_hi),
        out_shape=outs,
        in_specs=[pl.BlockSpec(memory_space=pltpu.SMEM)] + anywhere(4) + vmem(4) + anywhere(2) + vmem(2),
        out_specs=tuple(anywhere(4)),
        scratch_shapes=[
            whole,
            whole,
            pltpu.VMEM((Y_LO, half, width), BF16),
            pltpu.VMEM((Y_LO, half, width), BF16),
            pltpu.VMEM((Y_LO, 8, half), F32),
            narrow,
            narrow,
            pltpu.VMEM((stored, rows, width), BF16),
            pltpu.VMEM((stored, rows, width), BF16),
            narrow,
            pltpu.VMEM((rows, hidden_all), BF16),
            pltpu.VMEM((rows, hidden_all), BF16),
            narrow,
            narrow,
            narrow,
            narrow,
            wide,
            wide,
            pltpu.VMEM((rows, hidden_all), F32),
            wide,
            pltpu.VMEM((rows, 128), F32),
            wide,
            pltpu.VMEM((y_n, z_n, rows, features), BF16),
            pltpu.VMEM((y_n, z_n, rows, hidden), BF16),
            pltpu.VMEM((y_n, z_n, rows, hidden), BF16),
            pltpu.VMEM((y_n, z_n, rows, features), BF16),
            pltpu.VMEM((features, hidden), F32),
            pltpu.VMEM((features, hidden), F32),
            dma((8,)),
            pltpu.SemaphoreType.REGULAR,
            dma((2,)),
            dma((2, 2)),
            dma((2, 2)),
            dma((2,)),
            dma((2,)),
            dma((n_rings, 2, rounds)),
            dma((n_rings, 2, rounds)),
            dma((2, y_hi)),
            dma((2, y_hi)),
        ],
        compiler_params=pltpu.CompilerParams(
            collective_id=0, has_side_effects=True, vmem_limit_bytes=56 * 1024 * 1024
        ),
    )(
        sample_ids,
        embeddings,
        cotangent,
        w_up[0],
        w_down[0].T,
        b_up,
        b_down,
        ln_gain,
        ln_bias,
        fwd_store[0],
        bwd_store[0],
        fwd_scales[0].T,
        bwd_scales[0].T,
    )
    kept = pl.pallas_call(
        keep_kernel,
        out_shape=outs,
        in_specs=vmem(4),
        out_specs=tuple(vmem(4)),
    )(*results)
    return tuple(array[None] for array in kept)


def solution(mesh, y_hi=Y_HI):
    return jax.shard_map(
        functools.partial(per_device, mesh.shape["section"], mesh.shape["dp"], y_hi),
        mesh=mesh,
        in_specs=(
            P("dp", None),
            P("dp", None),
            P("section", "dp", "tensor"),
            P("section", "tensor", "dp"),
            P("section", "tensor"),
            P("section", None),
            P("section", None),
            P("section", None),
            P("section", "dp", None, None),
            P("section", "dp", None, None),
            P("dp"),
            P("section", "dp", None),
            P("section", "dp", None),
        ),
        out_specs=(
            P("section", "dp", None),
            P("section", "dp", None),
            P("section", "dp", "tensor"),
            P("section", "dp", "tensor"),
        ),
        check_vma=False,
    )
```

```python
import functools

import jax
import jax.numpy as jnp
from jax import lax
from jax.experimental import pallas as pl
from jax.experimental.pallas import tpu as pltpu
from jax.sharding import PartitionSpec as P

MESH = pl.DeviceIdType.MESH
BF16 = jnp.bfloat16
F32 = jnp.float32
Y_LO = 2
Y_HI = 4
TURN = 24

root_half = 0.7071067811865476
density = 0.3989422804014327
epsilon = 1e-05


class Place:
    def __init__(self, n_dp, y_hi=Y_HI):
        self.y_hi_n = y_hi
        self.z_n = n_dp // y_hi
        self.y_n = y_hi * Y_LO
        self.dp = lax.axis_index("dp")
        self.lo = lax.axis_index("tensor")
        self.hi = self.dp // self.z_n
        self.z = self.dp % self.z_n
        self.y = self.hi * Y_LO + self.lo

    def at_y(self, y):
        return {"dp": (y // Y_LO) * self.z_n + self.z, "tensor": y % Y_LO}

    def at_z(self, z):
        return {"dp": self.hi * self.z_n + z, "tensor": self.lo}

    def step_y(self, d):
        return (self.y + d + self.y_n) % self.y_n

    def step_z(self, d):
        return (self.z + d + self.z_n) % self.z_n


def signal(barrier, device_id):
    pl.semaphore_signal(barrier, inc=1, device_id=device_id, device_id_type=MESH)


def remote(src, dst, send_sem, recv_sem, device_id):
    return pltpu.make_async_remote_copy(
        src_ref=src, dst_ref=dst, send_sem=send_sem, recv_sem=recv_sem, device_id=device_id, device_id_type=MESH
    )


class Ring:
    def __init__(self, n, step, slot, device, sems, index, last_way):
        self.step, self.slot, self.device = step, slot, device
        self.send_sem, self.recv_sem, self.index = sems[0], sems[1], index
        self.rounds = n // 2
        self.last_way = last_way

    def ways(self, r):
        return (self.last_way,) if r == self.rounds - 1 else (0, 1)

    def copy(self, way, r, received=False):
        sign = 1 - 2 * way
        block = self.slot(self.step(-sign * (r + 1 if received else r)))
        spot = (self.index, way, r)
        return remote(block, block, self.send_sem.at[spot], self.recv_sem.at[spot], self.device(self.step(sign)))

    def start(self, r):
        for way in self.ways(r):
            self.copy(way, r).start()

    def wait_recv(self, r):
        for way in self.ways(r):
            self.copy(way, r, True).wait_recv()

    def wait_send(self):
        for r in range(self.rounds):
            for way in self.ways(r):
                self.copy(way, r).wait_send()


class Spread:
    def __init__(self, n, step, part, slot, device, sems, index):
        self.step, self.part, self.slot, self.device = step, part, slot, device
        self.send_sem, self.recv_sem, self.index = sems[0], sems[1], index
        self.rounds = n // 2

    def ways(self, r):
        return (0,) if r == self.rounds - 1 else (0, 1)

    def copy(self, way, r, received=False):
        sign = 1 - 2 * way
        spot = (self.index, way, r)
        target = self.step(sign * (r + 1))
        block = self.slot(self.step(-sign * (r + 1) if received else 0))
        source = block if received else self.part(target)
        return remote(source, block, self.send_sem.at[spot], self.recv_sem.at[spot], self.device(target))

    wait_send = Ring.wait_send


def start_spreads(pairs):
    for r in range(max(pair[1].rounds for pair in pairs)):
        for pair in pairs:
            if r < pair[1].rounds:
                for way in pair[1].ways(r):
                    pair[1].copy(way, r).start()


def run_gathers(pairs, lag=1.0, midway=None):
    free, events, count, missing, brought = {}, [], [0], {}, {}

    def push(ready, axis, ring, way, r, pair, size=1.0):
        begin = max(ready, free.get((axis, way), 0.0))
        free[axis, way] = begin + size
        count[0] += 1
        events.append((begin + size + lag, count[0], ring, way, r, pair))

    def go(ready, axis, ring, way, r, pair):
        push(ready, axis, ring, way, r, pair)
        ring.copy(way, r).start()

    def begin_chunk(ready, pair, d):
        for way in pair[3][d].ways(0):
            go(ready, pair[2], pair[3][d], way, 0, pair)

    def arrived(pair, n, d):
        key = (id(pair), d if d * 2 > -n else d + n)
        missing[key] = missing.get(key, len(pair[3])) - 1
        if missing[key] == 0 and pair[4] is not None:
            pair[4](d)

    for pair in pairs:
        spread = isinstance(pair[1], Spread)
        for r in range(pair[1].rounds if spread else 1):
            for way in pair[1].ways(r):
                if spread:
                    push(0.0, pair[0], pair[1], way, r, pair, r + 1.0)
                else:
                    go(0.0, pair[0], pair[1], way, r, pair)
    for pair in pairs:
        begin_chunk(0.0, pair, 0)
        arrived(pair, 2 * pair[3][0].rounds, 0)
    arrivals = 0
    while events:
        event = min(events, key=lambda e: e[:2])
        events.remove(event)
        now, _, ring, way, r, pair = event
        ring.copy(way, r, True).wait_recv()
        d = -(r + 1) if way == 0 else r + 1
        arrivals += 1
        if midway is not None and arrivals == midway[0]:
            midway[1]()
        first = ring is pair[1]
        if not (first and isinstance(ring, Spread)) and r + 1 < ring.rounds and way in ring.ways(r + 1):
            go(now, pair[0] if first else pair[2], ring, way, r + 1, pair)
        if first:
            begin_chunk(now, pair, d)
            arrived(pair, 2 * pair[3][0].rounds, 0)
        else:
            arrived(pair, 2 * ring.rounds, d)


def gelu_value(pre_gelu):
    return pre_gelu * 0.5 * (1.0 + lax.erf(pre_gelu * root_half))


def gelu_slope(pre_gelu):
    return (
        0.5 * (1.0 + lax.erf(pre_gelu * root_half))
        + pre_gelu * jnp.exp(-0.5 * pre_gelu * pre_gelu) * density
    )


def outer_t(left, right):
    return lax.dot_general(left, right, (((1,), (1,)), ((), ())), preferred_element_type=F32)


def inner(left, right):
    return lax.dot_general(left, right, (((0,), (0,)), ((), ())), preferred_element_type=F32)


def coded(values, base, bound):
    base = base.astype(F32)
    return (base + jnp.clip(values.astype(F32) - base, -bound, bound)).astype(BF16)


def layer_kernel(
    n_sections,
    n_dp,
    y_hi,
    sid_ref,
    emb_ref,
    cot_ref,
    up_ref,
    down_ref,
    bup_ref,
    bdown_ref,
    gain_ref,
    bias_ref,
    fst_ref,
    bst_ref,
    fsc_ref,
    bsc_ref,
    out_ref,
    ig_ref,
    up_out,
    down_out,
    up_all,
    down_all,
    up_turned,
    down_turned,
    bias_all,
    x_in,
    g_in,
    fst,
    bst,
    normed,
    act,
    pre_grad,
    out_rows,
    ig_rows,
    code_f,
    code_b,
    bound_f,
    bound_b,
    slope,
    unit,
    inv,
    scaled,
    normed_all,
    act_all,
    pg_all,
    g_all,
    up_block,
    down_block,
    load_sem,
    turn_sem,
    bias_sem,
    hop_send,
    hop_recv,
    peer_send,
    peer_recv,
    ring_send,
    ring_recv,
    out_send,
    out_recv,
):
    at = Place(n_dp, y_hi)
    section = lax.axis_index("section")
    rows, width = x_in.shape
    half = up_all.shape[2]
    features = normed_all.shape[3]
    hidden = act_all.shape[3]
    shard = up_ref.shape[0]
    wide = width // 2
    sems = (ring_send, ring_recv)
    mine = pl.ds(pl.multiple_of(at.lo * rows, rows), rows)
    other = pl.ds(pl.multiple_of((1 - at.lo) * rows, rows), rows)
    not_first = section > 0
    not_last = section < n_sections - 1
    early_first = section < n_sections // 2
    early_after = jnp.logical_not(early_first)
    after = {"section": jnp.minimum(section + 1, n_sections - 1)}
    before = {"section": jnp.maximum(section - 1, 0)}
    peer = {"tensor": 1 - at.lo}
    owner_z = at.dp // at.y_hi_n

    barrier = pltpu.get_barrier_semaphore()
    for d in range(1, at.y_n):
        signal(barrier, at.at_y(at.step_y(d)))
    for d in range(1, at.z_n):
        signal(barrier, at.at_z(at.step_z(d)))
    for i in range(at.y_hi_n):
        source = i * at.z_n + owner_z

        @pl.when(source != at.dp)
        def _():
            signal(barrier, {"dp": source})

    @pl.when(not_first)
    def _():
        signal(barrier, before)

    @pl.when(not_last)
    def _():
        signal(barrier, after)

    own_rows = pl.ds(pl.multiple_of(at.dp * shard, shard), shard)
    own_up = pltpu.make_async_copy(up_ref, up_all.at[at.lo, own_rows], load_sem.at[0])
    own_down = pltpu.make_async_copy(down_ref, down_all.at[at.lo, own_rows], load_sem.at[1])
    load_fst = pltpu.make_async_copy(fst_ref.at[:, mine], fst, load_sem.at[2])
    load_bst = pltpu.make_async_copy(bst_ref.at[:, mine], bst, load_sem.at[3])
    load_emb = pltpu.make_async_copy(emb_ref.at[mine], x_in, load_sem.at[4])
    load_cot = pltpu.make_async_copy(cot_ref.at[mine], g_in, load_sem.at[5])
    own_up.start()
    own_down.start()
    load_fst.start()
    load_bst.start()

    @pl.when(section == 0)
    def _():
        load_emb.start()

    @pl.when(jnp.logical_not(not_last))
    def _():
        load_cot.start()

    bias_all[at.lo] = jnp.broadcast_to(bup_ref[...], bias_all.shape[1:])
    sends_self = jnp.int32(0)
    for i in range(at.y_hi_n):
        sends_self = sends_self + (at.z * at.y_hi_n + i == at.dp).astype(jnp.int32)
    sections_near = not_first.astype(jnp.int32) + not_last.astype(jnp.int32)
    own_up.wait()
    own_down.wait()
    pl.semaphore_wait(barrier, at.y_n + at.z_n - 2 + at.y_hi_n - sends_self + sections_near)

    bias_copy = remote(bias_all.at[at.lo], bias_all.at[at.lo], bias_sem.at[0], bias_sem.at[1], peer)
    bias_copy.start()

    def shard_rows(y, z):
        return pl.ds(pl.multiple_of(((y // Y_LO) * at.z_n + z) * shard, shard), shard)

    def up_slot(y, z):
        return up_all.at[y % Y_LO, shard_rows(y, z)]

    def down_slot(y, z):
        return down_all.at[y % Y_LO, shard_rows(y, z)]

    def fixed(slot, axis, step, d):
        there = step(d)
        return (lambda z: slot(there, z)) if axis == "y" else (lambda y: slot(y, there))

    y_ring = (at.y_n, at.step_y)
    z_ring = (at.z_n, at.step_z)
    up_first = Ring(*y_ring, fixed(up_slot, "z", at.step_z, 0), at.at_y, sems, 0, 0)
    down_first = Ring(*z_ring, fixed(down_slot, "y", at.step_y, 0), at.at_z, sems, 1, 1)
    up_then, down_then = {}, {}
    index = 2
    for d in range(-(at.y_n // 2), at.y_n // 2):
        up_then[d] = Ring(*z_ring, fixed(up_slot, "y", at.step_y, d), at.at_z, sems, index, index % 2)
        index += 1
    for d in range(-(at.z_n // 2), at.z_n // 2):
        down_then[d] = Ring(*y_ring, fixed(down_slot, "z", at.step_z, d), at.at_y, sems, index, index % 2)
        index += 1
    if down_first.last_way == 1:
        down_then[at.z_n // 2] = down_then.pop(-(at.z_n // 2))
    weight_rings = [up_first, down_first, *up_then.values(), *down_then.values()]
    weight_pairs = (("y", up_first, "z", up_then, None), ("z", down_first, "y", down_then, None))
    even = section % 2 == 0

    @pl.when(jnp.logical_not(even))
    def _():
        pl.semaphore_wait(turn_sem, 1)

    def pass_turn():
        @pl.when(jnp.logical_and(even, not_last))
        def _():
            pl.semaphore_signal(turn_sem, inc=1, device_id=after, device_id_type=MESH)

    run_gathers(weight_pairs, midway=(TURN, pass_turn))

    scale_f = jnp.transpose(fsc_ref[...].astype(F32))
    scale_b = jnp.transpose(bsc_ref[...].astype(F32))
    low = at.lo == 0
    scale_f = 0.25 * jnp.where(low, scale_f[:rows], scale_f[rows:])
    scale_b = 0.25 * jnp.where(low, scale_b[:rows], scale_b[rows:])
    for b in range(fsc_ref.shape[0]):
        block = width // fsc_ref.shape[0]
        cols = pl.ds(b * block, block)
        bound_f[:, cols] = jnp.broadcast_to(scale_f[:, b : b + 1], (rows, block))
        bound_b[:, cols] = jnp.broadcast_to(scale_b[:, b : b + 1], (rows, block))
    remote(bias_all.at[1 - at.lo], bias_all.at[1 - at.lo], bias_sem.at[0], bias_sem.at[1], peer).wait_recv()
    bias_copy.wait_send()
    load_fst.wait()
    load_bst.wait()
    sid = sid_ref[0]

    def columns(j):
        return pl.ds(pl.multiple_of(j * wide, wide), wide)

    def fwd_copy(j):
        return remote(code_f.at[:, columns(j)], x_in.at[:, columns(j)], hop_send.at[0, j], hop_recv.at[0, j], after)

    def bwd_copy(j):
        return remote(code_b.at[:, columns(j)], g_in.at[:, columns(j)], hop_send.at[1, j], hop_recv.at[1, j], before)

    def hidden_half(h):
        return pl.ds(pl.multiple_of(h * half, half), half)

    def feature_cols(z):
        return pl.ds(pl.multiple_of(z * features, features), features)

    def hidden_cols(y):
        spot = (y % Y_LO) * at.y_hi_n + y // Y_LO
        return pl.ds(pl.multiple_of(spot * hidden, hidden), hidden)

    def exchange(src, dst, along_z, index, done=None):
        if along_z:
            spread = Spread(*z_ring, lambda z: src.at[:, feature_cols(z)], lambda z: dst.at[at.y, z], at.at_z, sems, index)
            there, ring, device = at.step_z, y_ring, at.at_y
        else:
            spread = Spread(*y_ring, lambda y: src.at[:, hidden_cols(y)], lambda y: dst.at[y, at.z], at.at_y, sems, index)
            there, ring, device = at.step_y, z_ring, at.at_z
        n = z_ring[0] if along_z else y_ring[0]
        rings = {}
        for d in range(1 - n // 2, n // 2 + 1):
            index += 1

            def slot(i, d=d):
                return dst.at[i, there(d)] if along_z else dst.at[there(d), i]

            rings[d if d < n // 2 else -d] = Ring(*ring, slot, device, sems, index, index % 2)
        axes = ("z", "y") if along_z else ("y", "z")
        return (axes[0], spread, axes[1], rings, done)

    def keep_own(src, dst, along_z):
        dst[at.y, at.z] = src[:, feature_cols(at.z)] if along_z else src[:, hidden_cols(at.y)]

    def add_column(d):
        z = at.step_z(d)
        left = normed_all[:, z].reshape(at.y_n * rows, features)
        up_block[...] += inner(left, pg_all[:, z].reshape(at.y_n * rows, hidden))

    def add_row(d):
        y = at.step_y(d)
        left = g_all[y].reshape(at.z_n * rows, features)
        down_block[...] += inner(left, act_all[y].reshape(at.z_n * rows, hidden))

    act_pair = exchange(act, act_all, False, index)
    normed_pair = exchange(normed, normed_all, True, index + 1 + at.y_n)
    pg_pair = exchange(pre_grad, pg_all, False, index + 2 + at.y_n + at.z_n, add_column)
    g_pair = exchange(g_in, g_all, True, index + 3 + 2 * at.y_n + at.z_n, add_row)
    early_pairs, late_pairs = (act_pair, normed_pair), (pg_pair, g_pair)

    def wait_sends(pairs):
        for pair in pairs:
            for ring in (pair[1], *pair[3].values()):
                ring.wait_send()

    def early_spreads():
        start_spreads(early_pairs)
        keep_own(act, act_all, False)
        keep_own(normed, normed_all, True)

    def early_sends():
        for ring in weight_rings:
            ring.wait_send()
        wait_sends(early_pairs)

    def turn(source, target):
        count = half // 128

        def body(i, _):
            cols = pl.ds(pl.multiple_of((i % count) * 128, 128), 128)
            target[i // count, cols, :] = jnp.transpose(source[i // count, :, cols])
            return 0

        lax.fori_loop(0, 2 * count, body, 0)

    @pl.when(not_first)
    def _():
        turn(down_all, down_turned)

    @pl.when(section > 1)
    def _():
        turn(up_all, up_turned)

    @pl.when(not_first)
    def _():
        for j in range(2):
            fwd_copy(j).wait_recv()

    @pl.when(section == 0)
    def _():
        load_emb.wait()

    values = x_in[...].astype(F32)
    centered = values - jnp.mean(values, axis=-1, keepdims=True)
    inverse = lax.rsqrt(jnp.mean(centered * centered, axis=-1, keepdims=True) + epsilon)
    unit_values = centered * inverse
    normed[...] = (unit_values * gain_ref[...] + bias_ref[...]).astype(BF16)
    unit[...] = unit_values
    inv[...] = jnp.broadcast_to(inverse, inv.shape)

    for h in range(2):
        spot = pl.ds(h * half, half)
        pre = jnp.dot(normed[...], up_all[h], preferred_element_type=F32) + bias_all[h, 0:1, :]
        slope[:, spot] = pre
        act[:, spot] = gelu_value(pre).astype(BF16)

    def finish_output(j, total):
        cols = pl.ds(j * wide, wide)
        output = (x_in[:, cols].astype(F32) + total + bdown_ref[:, cols]).astype(BF16)
        out_rows[:, cols] = output
        code_f[:, cols] = coded(output, fst[sid, :, cols], bound_f[:, cols])

        @pl.when(not_last)
        def _():
            fwd_copy(j).start()

    def product_t(left, right, j):
        cols = pl.ds(j * wide, wide)
        return outer_t(left[:, :half], right[0, cols, :]) + outer_t(left[:, half:], right[1, cols, :])

    def product(left, right, j):
        cols = pl.ds(j * wide, wide)
        return jnp.dot(left[:, :half], right[0, :, cols], preferred_element_type=F32) + jnp.dot(
            left[:, half:], right[1, :, cols], preferred_element_type=F32
        )

    @pl.when(section == 0)
    def _():
        for j in range(2):
            finish_output(j, product_t(act, down_all, j))

    @pl.when(not_first)
    def _():
        for j in range(2):
            finish_output(j, product(act, down_turned, j))

    out_keep = pltpu.make_async_copy(out_rows, out_ref.at[mine], load_sem.at[6])
    out_keep.start()
    out_copy = remote(out_rows, out_ref.at[mine], peer_send.at[0], peer_recv.at[0], peer)
    out_copy.start()

    @pl.when(section <= 1)
    def _():
        turn(up_all, up_turned)

    def slope_half(h, _):
        slope[:, hidden_half(h)] = gelu_slope(slope[:, hidden_half(h)])
        return 0

    lax.fori_loop(0, 2, slope_half, 0)

    @pl.when(jnp.logical_or(early_first, not_last))
    def _():
        early_spreads()

    @pl.when(early_first)
    def _():
        run_gathers(early_pairs)
        early_sends()

    @pl.when(not_last)
    def _():
        for j in range(2):
            bwd_copy(j).wait_recv()

    @pl.when(jnp.logical_not(not_last))
    def _():
        load_cot.wait()

    for h in range(2):
        spot = pl.ds(h * half, half)
        act_grad = jnp.dot(g_in[...], down_all[h], preferred_element_type=F32)
        pre_grad[:, spot] = (act_grad * slope[:, spot]).astype(BF16)

    def late_spreads():
        start_spreads(late_pairs)
        keep_own(pre_grad, pg_all, False)
        keep_own(g_in, g_all, True)

    @pl.when(section == 0)
    def _():
        late_spreads()

    for j in range(2):
        cols = pl.ds(j * wide, wide)
        scaled[:, cols] = product(pre_grad, up_turned, j) * gain_ref[:, cols]
    scaled_values = scaled[...]
    unit_values = unit[...]
    first_mean = jnp.mean(scaled_values, axis=-1, keepdims=True)
    second_mean = jnp.mean(scaled_values * unit_values, axis=-1, keepdims=True)

    for j in range(2):
        cols = pl.ds(j * wide, wide)
        inner_part = scaled[:, cols] - first_mean - unit[:, cols] * second_mean
        input_grad = (g_in[:, cols].astype(F32) + inv[:, 0:1] * inner_part).astype(BF16)
        ig_rows[:, cols] = input_grad
        code_b[:, cols] = coded(input_grad, bst[sid, :, cols], bound_b[:, cols])

        @pl.when(not_first)
        def _():
            bwd_copy(j).start()

    @pl.when(not_first)
    def _():
        late_spreads()

    ig_keep = pltpu.make_async_copy(ig_rows, ig_ref.at[mine], load_sem.at[7])
    ig_keep.start()
    ig_copy = remote(ig_rows, ig_ref.at[mine], peer_send.at[1], peer_recv.at[1], peer)
    ig_copy.start()

    @pl.when(jnp.logical_and(early_after, jnp.logical_not(not_last)))
    def _():
        early_spreads()

    up_block[...] = jnp.zeros_like(up_block)
    down_block[...] = jnp.zeros_like(down_block)
    @pl.when(early_first)
    def _():
        run_gathers(late_pairs)

    @pl.when(early_after)
    def _():
        run_gathers([pair[:4] + (None,) for pair in late_pairs + early_pairs])
        lax.fori_loop(0, at.z_n, lambda d, _: (add_column(d), 0)[1], 0)
        lax.fori_loop(0, at.y_n, lambda d, _: (add_row(d), 0)[1], 0)
        early_sends()

    out_cols = pl.ds(pl.multiple_of(at.hi * hidden, hidden), hidden)
    outs = ((0, up_block, up_out), (1, down_block, down_out))

    def grad_copy(k, block, out, i):
        return remote(
            block.at[pl.ds(i * shard, shard)],
            out.at[:, out_cols],
            out_send.at[k, i],
            out_recv.at[k, at.hi],
            {"dp": at.z * at.y_hi_n + i},
        )

    def grad_keep(k, block, out, i):
        return pltpu.make_async_copy(block.at[pl.ds(i * shard, shard)], out.at[:, out_cols], out_send.at[k, i])

    for i in range(at.y_hi_n):
        own = at.z * at.y_hi_n + i == at.dp

        @pl.when(jnp.logical_not(own))
        def _():
            for k, block, out in outs:
                grad_copy(k, block, out, i).start()

        @pl.when(own)
        def _():
            for k, block, out in outs:
                grad_keep(k, block, out, i).start()

    @pl.when(not_last)
    def _():
        for j in range(2):
            fwd_copy(j).wait_send()

    @pl.when(not_first)
    def _():
        for j in range(2):
            bwd_copy(j).wait_send()

    wait_sends(late_pairs)
    remote(out_rows, out_ref.at[other], peer_send.at[0], peer_recv.at[0], peer).wait_recv()
    remote(ig_rows, ig_ref.at[other], peer_send.at[1], peer_recv.at[1], peer).wait_recv()
    out_copy.wait_send()
    ig_copy.wait_send()
    out_keep.wait()
    ig_keep.wait()

    for i in range(at.y_hi_n):

        @pl.when(i * at.z_n + owner_z != at.dp)
        def _():
            for k, block, out in outs:
                spot = out.at[:, pl.ds(i * hidden, hidden)]
                remote(spot, spot, out_send.at[k, 0], out_recv.at[k, i], {"dp": at.z * at.y_hi_n + i}).wait_recv()

    for i in range(at.y_hi_n):
        own = at.z * at.y_hi_n + i == at.dp

        @pl.when(jnp.logical_not(own))
        def _():
            for k, block, out in outs:
                grad_copy(k, block, out, i).wait_send()

        @pl.when(own)
        def _():
            for k, block, out in outs:
                grad_keep(k, block, out, i).wait()


def keep_kernel(*refs):
    count = len(refs) // 2
    for source, target in zip(refs[:count], refs[count:]):
        target[...] = source[...]


def vmem(count):
    return [pl.BlockSpec(memory_space=pltpu.VMEM)] * count


def anywhere(count):
    return [pl.BlockSpec(memory_space=pl.ANY)] * count


def per_device(
    n_sections,
    n_dp,
    y_hi,
    embeddings,
    cotangent,
    w_up,
    w_down,
    b_up,
    b_down,
    ln_gain,
    ln_bias,
    fwd_store,
    bwd_store,
    sample_ids,
    fwd_scales,
    bwd_scales,
):
    z_n = n_dp // y_hi
    y_n = y_hi * Y_LO
    shard, half = w_up.shape[1:]
    width = embeddings.shape[1]
    rows = embeddings.shape[0] // Y_LO
    hidden_all = Y_LO * half
    features = width // z_n
    hidden = hidden_all // y_n
    stored = fwd_store.shape[1]
    dma = pltpu.SemaphoreType.DMA
    rounds = max(y_n, z_n) // 2
    n_rings = 6 + 3 * (y_n + z_n)
    whole = pltpu.VMEM((Y_LO, width, half), BF16)
    narrow = pltpu.VMEM((rows, width), BF16)
    wide = pltpu.VMEM((rows, width), F32)
    outs = (
        jax.ShapeDtypeStruct(embeddings.shape, BF16),
        jax.ShapeDtypeStruct(embeddings.shape, BF16),
        jax.ShapeDtypeStruct((shard, half), F32),
        jax.ShapeDtypeStruct((shard, half), F32),
    )
    results = pl.pallas_call(
        functools.partial(layer_kernel, n_sections, n_dp, y_hi),
        out_shape=outs,
        in_specs=[pl.BlockSpec(memory_space=pltpu.SMEM)] + anywhere(4) + vmem(4) + anywhere(2) + vmem(2),
        out_specs=tuple(anywhere(4)),
        scratch_shapes=[
            whole,
            whole,
            pltpu.VMEM((Y_LO, half, width), BF16),
            pltpu.VMEM((Y_LO, half, width), BF16),
            pltpu.VMEM((Y_LO, 8, half), F32),
            narrow,
            narrow,
            pltpu.VMEM((stored, rows, width), BF16),
            pltpu.VMEM((stored, rows, width), BF16),
            narrow,
            pltpu.VMEM((rows, hidden_all), BF16),
            pltpu.VMEM((rows, hidden_all), BF16),
            narrow,
            narrow,
            narrow,
            narrow,
            wide,
            wide,
            pltpu.VMEM((rows, hidden_all), F32),
            wide,
            pltpu.VMEM((rows, 128), F32),
            wide,
            pltpu.VMEM((y_n, z_n, rows, features), BF16),
            pltpu.VMEM((y_n, z_n, rows, hidden), BF16),
            pltpu.VMEM((y_n, z_n, rows, hidden), BF16),
            pltpu.VMEM((y_n, z_n, rows, features), BF16),
            pltpu.VMEM((features, hidden), F32),
            pltpu.VMEM((features, hidden), F32),
            dma((8,)),
            pltpu.SemaphoreType.REGULAR,
            dma((2,)),
            dma((2, 2)),
            dma((2, 2)),
            dma((2,)),
            dma((2,)),
            dma((n_rings, 2, rounds)),
            dma((n_rings, 2, rounds)),
            dma((2, y_hi)),
            dma((2, y_hi)),
        ],
        compiler_params=pltpu.CompilerParams(
            collective_id=0, has_side_effects=True, vmem_limit_bytes=56 * 1024 * 1024
        ),
    )(
        sample_ids,
        embeddings,
        cotangent,
        w_up[0],
        w_down[0].T,
        b_up,
        b_down,
        ln_gain,
        ln_bias,
        fwd_store[0],
        bwd_store[0],
        fwd_scales[0].T,
        bwd_scales[0].T,
    )
    kept = pl.pallas_call(
        keep_kernel,
        out_shape=outs,
        in_specs=vmem(4),
        out_specs=tuple(vmem(4)),
    )(*results)
    return tuple(array[None] for array in kept)


def solution(mesh, y_hi=Y_HI):
    return jax.shard_map(
        functools.partial(per_device, mesh.shape["section"], mesh.shape["dp"], y_hi),
        mesh=mesh,
        in_specs=(
            P("dp", None),
            P("dp", None),
            P("section", "dp", "tensor"),
            P("section", "tensor", "dp"),
            P("section", "tensor"),
            P("section", None),
            P("section", None),
            P("section", None),
            P("section", "dp", None, None),
            P("section", "dp", None, None),
            P("dp"),
            P("section", "dp", None),
            P("section", "dp", None),
        ),
        out_specs=(
            P("section", "dp", None),
            P("section", "dp", None),
            P("section", "dp", "tensor"),
            P("section", "dp", "tensor"),
        ),
        check_vma=False,
    )
```
